512 devices in a mesh: dp: 16 (over z, x_hi), vocab: 32 (over x_lo, y, core).
Axes of the slice: x: 4 (x_hi: 2, x_lo: 2; x = x_hi * 2 + x_lo), y: 8, z: 8, core: 2. Of those that a mesh axis runs over, the one named last changes fastest.
Arguments:
- hidden: bfloat16 [1024, 4608], P('dp'), may hold values from -300 to 300
- labels: int32 [1024], P('dp'), may hold values from 0 to 131071
- unembed: bfloat16 [4608, 131072], P(None, ('dp', 'vocab')), may hold values from -0.09375 to 0.09375
- in_proj: bfloat16 [4608, 64], replicated, may hold values from -0.09375 to 0.09375
- out_proj: float32 [131072, 64], P(('dp', 'vocab')), may hold values from -6 to 6
- left_inv: float32 [64, 64], replicated, may hold values from -1 to 4
- right_inv: float32 [64, 64], replicated, may hold values from -1 to 4
- queries: float32 [16, 256, 4096], P('dp', 'vocab'), may hold values from -0.012 to 0.012
Outputs:
- scores: float32 [16, 16, 256], P('dp', None, 'vocab')
The draws below stay inside these ranges and needn't reach their ends.
All inputs are finite; a program needn't handle non-finite values.
Results may differ from the reference program's by a relative error of at most 0.00065.
Values may be sent and summed in bfloat16 or wider, within the bound.
No kernel may reach another device: no remote copies, remote signals or barrier semaphores. Data moves between devices by JAX's collectives and lax.ppermute only.
A program may use at most 128 MiB of HBM per device.

```python
import math
import jax
import jax.numpy as jnp
from jax import lax

D = 4608
VOCAB = 131072
RANK = 64
LEN = 64
TOKENS = 1024
QGROUPS = 16
QROWS = 256
FEAT = 4096
N_DP = 16


def factor_matrix(key):
    first_key, second_key = jax.random.split(key)
    diagonal = jax.random.uniform(first_key, (RANK,), jnp.float32, 1.0, 3.0)
    spread = jax.random.uniform(second_key, (RANK, RANK), jnp.float32, -1.0, 1.0) * (2.0 / RANK)
    return jnp.diag(diagonal) + 0.5 * (spread + spread.T)


def draw_hidden(key, part):
    key = jax.random.fold_in(key, 11)
    first_key, second_key = jax.random.split(key)
    base = jnp.clip(jax.random.normal(first_key, (TOKENS, D), jnp.float32), -5.0, 5.0)
    scales = jnp.exp(jax.random.uniform(second_key, (TOKENS, 1), jnp.float32, 0.0, math.log(3.0)))
    return (base * scales).astype(jnp.bfloat16)


def draw_left_inv(key, part):
    key = jax.random.fold_in(key, 23)
    return factor_matrix(key)


def draw_right_inv(key, part):
    key = jax.random.fold_in(key, 37)
    return factor_matrix(key)


def touch_ends(drawn, own_key, smallest, top_value):
    index_at = [jax.random.randint(jax.random.fold_in(own_key, axis), (), 0, length) for axis, length in enumerate(drawn.shape)]
    main_axis = drawn.shape.index(max(drawn.shape))
    neighbour = index_at[:main_axis] + [(index_at[main_axis] + 1) % drawn.shape[main_axis]] + index_at[main_axis + 1:]
    return drawn.at[tuple(index_at)].set(smallest).at[tuple(neighbour)].set(top_value)


def level_of(own_key, shape, shards, least, high):
    def one(position, shards_of):
        heights = jax.random.uniform(jax.random.fold_in(jax.random.fold_in(own_key, 6), position), (shards_of,), jnp.float32, least / len(shards), high / len(shards))
        return jnp.repeat(jnp.exp(heights), shape[position] // shards_of).reshape((-1,) + (1,) * (len(shape) - position - 1))

    loudness = one(*shards[0])
    for cut in shards[1:]:
        loudness = loudness * one(*cut)
    return loudness


def noise(rng, dims, scale, most, cuts=(), kind=jnp.bfloat16):
    gain = level_of(rng, dims, cuts, -0.22, 0.18) if cuts else 1.0
    entries = jax.random.normal(rng, dims, jnp.float32) * scale * gain
    return jnp.minimum(jnp.maximum(entries, -most), most).astype(kind)


def setup_inputs(seed: int = 0) -> dict:
    splits = jax.random.split(jax.random.key(seed), 9)
    hidden = draw_hidden(jax.random.fold_in(splits[8], 71), 0)
    labels = touch_ends(jax.random.randint(splits[1], (TOKENS,), 0, VOCAB), jax.random.fold_in(splits[1], 1), 0, VOCAB - 1).astype(jnp.int32)
    unembed = noise(splits[2], (D, VOCAB), D ** -0.5, 0.09375, ((1, 512),))
    in_proj = noise(splits[3], (D, RANK), D ** -0.5, 0.09375)
    out_proj = noise(splits[4], (VOCAB, RANK), 1.0, 6.0, ((0, 512),), jnp.float32)
    left_inv = draw_left_inv(jax.random.fold_in(splits[8], 71), 0)
    right_inv = draw_right_inv(jax.random.fold_in(splits[8], 71), 0)
    queries = noise(splits[7], (QGROUPS, QROWS, FEAT), 0.002, 0.012, ((0, 16), (1, 32)), jnp.float32)
    return {"hidden": hidden, "labels": labels, "unembed": unembed, "in_proj": in_proj, "out_proj": out_proj, "left_inv": left_inv, "right_inv": right_inv, "queries": queries}


PRECISE = lax.Precision.HIGHEST


def reference(hidden, labels, unembed, in_proj, out_proj, left_inv, right_inv, queries):
    seq_hidden = hidden.reshape(N_DP, LEN, D)
    seq_labels = labels.reshape(N_DP, LEN)
    vocab_ids = jnp.arange(VOCAB, dtype=jnp.int32)
    block_cols = VOCAB // N_DP
    block_starts = jnp.arange(N_DP, dtype=jnp.int32) * block_cols
    proj_wide = in_proj.astype(jnp.float32)

    def sequence_features(inputs):
        rows_hidden, rows_labels = inputs
        rows_wide = rows_hidden.astype(jnp.float32)

        def block_logits(start):
            columns = lax.dynamic_slice_in_dim(unembed, start.astype(jnp.int32), block_cols, 1).astype(jnp.float32)
            return jnp.dot(rows_wide, columns, precision=PRECISE)

        pieces = lax.map(block_logits, block_starts)
        logits = jnp.transpose(pieces, (1, 0, 2)).reshape(LEN, VOCAB)
        largest = jnp.max(logits, axis=1, keepdims=True)
        exponent = jnp.exp(logits - largest)
        totals = jnp.sum(exponent, axis=1, keepdims=True)
        label_mask = (rows_labels.astype(jnp.int32)[:, None] == vocab_ids[None, :]).astype(jnp.float32)
        residual = exponent / totals - label_mask
        projected = jnp.dot(residual, out_proj, precision=PRECISE)
        mapped = jnp.dot(rows_wide, proj_wide, precision=PRECISE)
        feature = jnp.dot(mapped.T, projected, precision=PRECISE)
        return jnp.dot(jnp.dot(left_inv, feature, precision=PRECISE), right_inv, precision=PRECISE)

    precond = lax.map(sequence_features, (seq_hidden, seq_labels))
    flattened = precond.reshape(N_DP, RANK * RANK)
    return jnp.einsum("sf,jqf->sjq", flattened, queries, precision=PRECISE)
```

```python
import jax
import jax.numpy as jnp
from jax import lax
from jax.sharding import Mesh, PartitionSpec as P

PRECISE = lax.Precision.HIGHEST
EVERY = ("z", "xh", "xl", "yh", "yl", "core")
DP = ("z", "xh")
VOC = ("xl", "yh", "yl", "core")
SWAP = [(0, 1), (1, 0)]


def exchange(blocks, axes):
    return lax.all_to_all(blocks, axes, split_axis=0, concat_axis=0, tiled=True)


def spread_out(block, axes, count):
    return exchange(jnp.broadcast_to(block[None], (count,) + block.shape), axes)


def both_ways(value, axes, count):
    pairs = [(2 * i, 2 * ((i + 1) % count)) for i in range(count)]
    pairs += [(2 * i + 1, 2 * ((i - 1) % count) + 1) for i in range(count)]
    return lax.ppermute(value, axes + ("core",), pairs)


def local(hidden, labels, unembed, in_proj, out_proj, left_inv, right_inv, queries):
    core, xl, xh = lax.axis_index("core"), lax.axis_index("xl"), lax.axis_index("xh")
    y = lax.axis_index("yh") * 2 + lax.axis_index("yl")
    rows = 16 * (2 * lax.axis_index("yl") + core)
    z = lax.axis_index("z")

    chosen = lax.dynamic_slice(hidden, (rows, 2304 * xl), (16, 2304))
    picked = lax.dynamic_slice(labels, (rows,), (16,))
    digits = jnp.stack([picked // 65536, (picked // 256) % 256, picked % 256], axis=1)
    digits = jnp.pad(digits, ((0, 0), (0, 125))).astype(jnp.bfloat16)
    own0 = spread_out(jnp.concatenate([chosen[:, :1152], digits], axis=1), DP, 16).reshape(256, 1280)
    own1 = spread_out(chosen[:, 1152:], DP, 16).reshape(256, 1152)
    digits, own0 = own0[:, 1152:].astype(jnp.int32), own0[:, :1152]
    every_label = digits[:, 0:1] * 65536 + digits[:, 1:2] * 256 + digits[:, 2:3]
    rest0 = both_ways(own0, ("xh", "xl"), 4)
    rest1 = both_ways(own1, ("xh", "xl"), 4)

    query_pair = jnp.stack([queries[0], lax.ppermute(queries[0], "xh", SWAP)])
    query_pair, _ = lax.optimization_barrier((query_pair, own0))
    every_query = lax.all_gather(query_pair, "z", axis=0)

    weights = [unembed, both_ways(unembed, ("yh", "yl"), 8)]
    weights += [lax.ppermute(block, "core", SWAP) for block in weights]
    tables = jnp.concatenate([out_proj, both_ways(out_proj, ("yh", "yl"), 8)], axis=0)
    table = jnp.concatenate([tables, lax.ppermute(tables, "core", SWAP)], axis=0)

    def block_start(at_y, at_core):
        return (((z * 2 + xh) * 2 + xl) * 16 + at_y * 2 + at_core) * 256

    below, above = (y + 7) % 8, (y + 1) % 8
    starts = [
        block_start(y, core),
        block_start(jnp.where(core == 0, below, above), core),
        block_start(y, 1 - core),
        block_start(jnp.where(core == 0, above, below), 1 - core),
    ]
    ids = lax.iota(jnp.int32, 256)
    column_ids = jnp.concatenate([start + ids for start in starts])
    mask = (every_label == column_ids[None, :]).astype(jnp.float32)
    label_rows = jnp.dot(mask, table, precision=PRECISE)
    mapped = jnp.dot(hidden, in_proj, preferred_element_type=jnp.float32)

    def product(values, weight, start):
        part = lax.dynamic_slice(weight, (start, 0), (1152, 256))
        return jnp.dot(values, part, preferred_element_type=jnp.float32)

    here, there = 2304 * xl, 2304 * (1 - xl)
    logits = [
        product(own0, weight, here)
        + product(own1, weight, here + 1152)
        + product(rest0, weight, there)
        + product(rest1, weight, there + 1152)
        for weight in weights
    ]
    logits = jnp.concatenate(logits, axis=1)
    largest = jnp.max(logits, axis=1, keepdims=True)
    exponent = jnp.exp(logits - largest)
    totals = jnp.sum(exponent, axis=1, keepdims=True)
    sums = jnp.dot(exponent, table, precision=PRECISE)

    ends = jnp.pad(jnp.concatenate([largest, totals], axis=1), ((0, 0), (0, 126)))
    packed = jnp.concatenate([sums, label_rows, ends], axis=1)

    def merge(parts, axis):
        sums, label_rows = parts[..., :64], parts[..., 64:128]
        largest, totals = parts[..., 128:129], parts[..., 129:130]
        top = jnp.max(largest, axis=axis, keepdims=True)
        scaled = jnp.exp(largest - top)
        sums = jnp.sum(sums * scaled, axis=axis)
        return sums, jnp.sum(label_rows, axis=axis), jnp.squeeze(top, axis), jnp.sum(totals * scaled, axis=axis)

    merged = merge(exchange(packed.reshape(32, 8, 256), ("z", "xh", "xl")), 0)
    packed = jnp.pad(jnp.concatenate(merged, axis=-1), ((0, 0), (0, 126)))
    parts = spread_out(packed, VOC, 32).reshape(2, 4, 2, 2, 8, 256)
    sums, label_rows, _, totals = merge(parts, 1)
    projected = sums / totals - label_rows
    projected = jnp.transpose(projected, (1, 2, 0, 3, 4)).reshape(64, 64)

    feature = jnp.dot(mapped.T, projected, precision=PRECISE)
    precond = jnp.dot(jnp.dot(left_inv, feature, precision=PRECISE), right_inv, precision=PRECISE)
    scores = jnp.sum(every_query * precond.reshape(1, 1, 1, 4096), axis=3)
    scores = jnp.where(xh == 0, scores, scores[:, ::-1])
    return scores.reshape(1, 16, 8)


def solution(mesh):
    fine = Mesh(mesh.devices.reshape(8, 2, 2, 4, 2, 2), EVERY)
    in_specs = (
        P(DP, None),
        P(DP),
        P(None, EVERY),
        P(),
        P(EVERY, None),
        P(),
        P(),
        P(DP, VOC, None),
    )
    out_specs = P(DP, None, VOC)
    return jax.shard_map(local, mesh=fine, in_specs=in_specs, out_specs=out_specs, check_vma=False)
```

```python
import jax
import jax.numpy as jnp
from jax import lax
from jax.experimental import pallas as pl
from jax.experimental.pallas import tpu as pltpu
from jax.sharding import Mesh, PartitionSpec as P

PRECISE = lax.Precision.HIGHEST
EVERY = ("zh", "zl", "xh", "xl", "yh", "yl", "core")
DP = ("zh", "zl", "xh")
VOC = ("xl", "yh", "yl", "core")
SWAP = [(0, 1), (1, 0)]
STEPS = 3
DEPTH = 2304 // STEPS
ROWS = 128


def exchange(blocks, axes):
    return lax.all_to_all(blocks, axes, split_axis=0, concat_axis=0, tiled=True)


def spread_out(block, axes, count):
    return exchange(jnp.broadcast_to(block[None], (count,) + block.shape), axes)


def both_ways(value, axes, count):
    pairs = [(2 * i, 2 * ((i + 1) % count)) for i in range(count)]
    pairs += [(2 * i + 1, 2 * ((i - 1) % count) + 1) for i in range(count)]
    return lax.ppermute(value, axes + ("core",), pairs)


def add_products(near_ref, far_ref, weight_refs, acc_ref):
    for block, weight in enumerate(weight_refs):
        columns = pl.ds(256 * block, 256)
        for start, rows in ((0, near_ref), (ROWS, far_ref)):
            acc_ref[pl.ds(start, ROWS), columns] += jnp.dot(
                rows[...], weight[...], preferred_element_type=jnp.float32
            )


def first_kernel(where_ref, near_ref, far_ref, w0, w1, w2, w3, acc_ref):
    @pl.when(pl.program_id(0) == 0)
    def _():
        acc_ref[...] = jnp.zeros_like(acc_ref)

    add_products(near_ref, far_ref, (w0, w1, w2, w3), acc_ref)


def last_kernel(where_ref, near_ref, far_ref, w0, w1, w2, w3, begun_ref, table_ref, label_ref, out_ref, acc_ref):
    step = pl.program_id(0)

    @pl.when(step == 0)
    def _():
        acc_ref[...] = begun_ref[...]

    add_products(near_ref, far_ref, (w0, w1, w2, w3), acc_ref)

    @pl.when(step == STEPS - 1)
    def _():
        logits = acc_ref[...]
        largest = jnp.max(logits, axis=1, keepdims=True)
        exponent = jnp.exp(logits - largest)
        totals = jnp.sum(exponent, axis=1, keepdims=True)
        sums = jnp.dot(exponent, table_ref[...], precision=PRECISE, preferred_element_type=jnp.float32)
        left = jnp.concatenate([sums, label_ref[...]], axis=1)
        lane = lax.broadcasted_iota(jnp.int32, (2 * ROWS, 128), 1)
        right = jnp.where(lane == 0, largest, jnp.where(lane == 1, totals, 0.0))
        parity = where_ref[1]
        for start, place in ((0, parity), (ROWS, 1 - parity)):
            out_ref[:, pl.ds(place, 1), :, 0:128] = left[start : start + ROWS].reshape(4, 1, 32, 128)
            out_ref[:, pl.ds(place, 1), :, 128:256] = right[start : start + ROWS].reshape(4, 1, 32, 128)


def product_specs():
    rows = pl.BlockSpec((ROWS, DEPTH), lambda step, where: (0, step))
    weight = pl.BlockSpec((DEPTH, 256), lambda step, where: (where[0] * STEPS + step, 0))
    return [rows, rows] + [weight] * 4


def whole(shape):
    return pl.BlockSpec(shape, lambda step, where: (0,) * len(shape))


COST = dict(flops=2 * 256 * 2304 * 1024, bytes_accessed=7_000_000)


def first_products(where, near, far, weights):
    return pl.pallas_call(
        first_kernel,
        out_shape=jax.ShapeDtypeStruct((256, 1024), jnp.float32),
        grid_spec=pltpu.PrefetchScalarGridSpec(
            num_scalar_prefetch=1,
            grid=(STEPS,),
            in_specs=product_specs(),
            out_specs=whole((256, 1024)),
        ),
        compiler_params=pltpu.CompilerParams(vmem_limit_bytes=24 << 20),
        cost_estimate=pl.CostEstimate(transcendentals=0, **COST),
    )(where, near, far, *weights)


def last_products(where, near, far, weights, begun, table, label_rows):
    return pl.pallas_call(
        last_kernel,
        out_shape=jax.ShapeDtypeStruct((4, 2, 32, 256), jnp.float32),
        grid_spec=pltpu.PrefetchScalarGridSpec(
            num_scalar_prefetch=1,
            grid=(STEPS,),
            in_specs=product_specs() + [whole((256, 1024)), whole((1024, 64)), whole((256, 64))],
            out_specs=whole((4, 2, 32, 256)),
            scratch_shapes=[pltpu.VMEM((256, 1024), jnp.float32)],
        ),
        compiler_params=pltpu.CompilerParams(vmem_limit_bytes=24 << 20),
        cost_estimate=pl.CostEstimate(transcendentals=256 * 1024, **COST),
    )(where, near, far, *weights, begun, table, label_rows)


def local(hidden, labels, unembed, in_proj, out_proj, left_inv, right_inv, queries):
    core, xl, xh, zl = [lax.axis_index(name) for name in ("core", "xl", "xh", "zl")]
    y = lax.axis_index("yh") * 2 + lax.axis_index("yl")
    rows = 16 * (2 * lax.axis_index("yl") + core)
    z = lax.axis_index("zh") * 2 + zl

    chosen = lax.dynamic_slice(hidden, (rows, 2304 * xl), (16, 2304))
    picked = lax.dynamic_slice(labels, (rows,), (16,))
    digits = jnp.stack([picked // 65536, (picked // 256) % 256, picked % 256], axis=1)
    digits = jnp.pad(digits, ((0, 0), (0, 125))).astype(jnp.bfloat16)
    chosen = jnp.concatenate([chosen, digits], axis=1)
    near = spread_out(chosen, ("zh", "xh"), 8).reshape(ROWS, 2432)
    far = both_ways(near, ("zh", "zl"), 8)
    near_x = both_ways(near, ("xh", "xl"), 4)
    far_x = both_ways(far, ("xh", "xl"), 4)

    query_pair = jnp.stack([queries[0], lax.ppermute(queries[0], "xh", SWAP)])
    query_pair, _ = lax.optimization_barrier((query_pair, near))
    every_query = lax.all_gather(query_pair, ("zh", "zl"), axis=0)

    weights = [unembed, both_ways(unembed, ("yh", "yl"), 8)]
    weights += [lax.ppermute(block, "core", SWAP) for block in weights]
    tables = jnp.concatenate([out_proj, both_ways(out_proj, ("yh", "yl"), 8)], axis=0)
    table = jnp.concatenate([tables, lax.ppermute(tables, "core", SWAP)], axis=0)

    def block_start(at_y, at_core):
        return (((z * 2 + xh) * 2 + xl) * 16 + at_y * 2 + at_core) * 256

    below, above = (y + 7) % 8, (y + 1) % 8
    starts = [
        block_start(y, core),
        block_start(jnp.where(core == 0, below, above), core),
        block_start(y, 1 - core),
        block_start(jnp.where(core == 0, above, below), 1 - core),
    ]
    ids = lax.iota(jnp.int32, 256)
    column_ids = jnp.concatenate([start + ids for start in starts])
    digits = jnp.concatenate([near[:, 2304:], far[:, 2304:]], axis=0).astype(jnp.int32)
    every_label = digits[:, 0:1] * 65536 + digits[:, 1:2] * 256 + digits[:, 2:3]
    mask = (every_label == column_ids[None, :]).astype(jnp.float32)
    label_rows = jnp.dot(mask, table, precision=PRECISE)
    mapped = jnp.dot(hidden, in_proj, preferred_element_type=jnp.float32)

    begun = first_products(jnp.stack([xl, zl]), near, far, weights)
    packed = last_products(jnp.stack([1 - xl, zl]), near_x, far_x, weights, begun, table, label_rows)

    def merge(parts, axis):
        sums, label_rows = parts[..., :64], parts[..., 64:128]
        largest, totals = parts[..., 128:129], parts[..., 129:130]
        top = jnp.max(largest, axis=axis, keepdims=True)
        scaled = jnp.exp(largest - top)
        sums = jnp.sum(sums * scaled, axis=axis)
        return sums, jnp.sum(label_rows, axis=axis), jnp.squeeze(top, axis), jnp.sum(totals * scaled, axis=axis)

    merged = merge(exchange(packed.reshape(32, 8, 256), ("zh", "zl", "xh", "xl")), 0)
    packed = jnp.pad(jnp.concatenate(merged, axis=-1), ((0, 0), (0, 126)))
    parts = spread_out(packed, VOC, 32).reshape(2, 4, 2, 2, 8, 256)
    sums, label_rows, _, totals = merge(parts, 1)
    projected = sums / totals - label_rows
    projected = jnp.transpose(projected, (1, 2, 0, 3, 4)).reshape(64, 64)

    feature = jnp.dot(mapped.T, projected, precision=PRECISE)
    precond = jnp.dot(jnp.dot(left_inv, feature, precision=PRECISE), right_inv, precision=PRECISE)
    scores = jnp.sum(every_query * precond.reshape(1, 1, 1, 4096), axis=3)
    scores = jnp.where(xh == 0, scores, scores[:, ::-1])
    return scores.reshape(1, 16, 8)


def solution(mesh):
    fine = Mesh(mesh.devices.reshape(4, 2, 2, 2, 4, 2, 2), EVERY)
    in_specs = (
        P(DP, None),
        P(DP),
        P(None, EVERY),
        P(),
        P(EVERY, None),
        P(),
        P(),
        P(DP, VOC, None),
    )
    out_specs = P(DP, None, VOC)
    return jax.shard_map(local, mesh=fine, in_specs=in_specs, out_specs=out_specs, check_vma=False)
```

```python
import functools
import jax
import jax.numpy as jnp
from jax import lax
from jax.experimental import pallas as pl
from jax.experimental.pallas import tpu as pltpu
from jax.sharding import Mesh, PartitionSpec as P

PRECISE = lax.Precision.HIGHEST
EVERY = ("zh", "zl", "xh", "xl", "yh", "yl", "core")
DP = ("zh", "zl", "xh")
VOC = ("xl", "yh", "yl", "core")
SWAP = [(0, 1), (1, 0)]
STEPS = 3
DEPTH = 2304 // STEPS
ROWS = 128


def exchange(blocks, axes):
    return lax.all_to_all(blocks, axes, split_axis=0, concat_axis=0, tiled=True)


def spread_out(block, axes, count):
    return exchange(jnp.broadcast_to(block[None], (count,) + block.shape), axes)


def both_ways(value, axes, count):
    pairs = [(2 * i, 2 * ((i + 1) % count)) for i in range(count)]
    pairs += [(2 * i + 1, 2 * ((i - 1) % count) + 1) for i in range(count)]
    return lax.ppermute(value, axes + ("core",), pairs)


def add_products(near_ref, far_ref, weight_refs, acc_ref):
    for block, weight in enumerate(weight_refs):
        columns = pl.ds(256 * block, 256)
        for start, rows in ((0, near_ref), (ROWS, far_ref)):
            acc_ref[pl.ds(start, ROWS), columns] += jnp.dot(
                rows[...], weight[...], preferred_element_type=jnp.float32
            )


def first_kernel(where_ref, near_ref, far_ref, w0, w1, w2, w3, acc_ref):
    @pl.when(pl.program_id(0) == 0)
    def _():
        acc_ref[...] = jnp.zeros_like(acc_ref)

    add_products(near_ref, far_ref, (w0, w1, w2, w3), acc_ref)


def last_kernel(where_ref, near_ref, far_ref, w0, w1, w2, w3, begun_ref, table_ref, label_ref, out_ref, acc_ref):
    step = pl.program_id(0)

    @pl.when(step == 0)
    def _():
        acc_ref[...] = begun_ref[...]

    add_products(near_ref, far_ref, (w0, w1, w2, w3), acc_ref)

    @pl.when(step == STEPS - 1)
    def _():
        logits = acc_ref[...]
        largest = jnp.max(logits, axis=1, keepdims=True)
        exponent = jnp.exp(logits - largest)
        totals = jnp.sum(exponent, axis=1, keepdims=True)
        sums = jnp.dot(exponent, table_ref[...], precision=PRECISE, preferred_element_type=jnp.float32)
        left = jnp.concatenate([sums, label_ref[...]], axis=1)
        lane = lax.broadcasted_iota(jnp.int32, (2 * ROWS, 128), 1)
        right = jnp.where(lane == 0, largest, jnp.where(lane == 1, totals, 0.0))
        parity = where_ref[1]
        for start, place in ((0, parity), (ROWS, 1 - parity)):
            out_ref[:, pl.ds(place, 1), :, 0:128] = left[start : start + ROWS].reshape(4, 1, 32, 128)
            out_ref[:, pl.ds(place, 1), :, 128:256] = right[start : start + ROWS].reshape(4, 1, 32, 128)


def merge_kernel(parts_ref, out_ref):
    left, right = parts_ref[:, :, 0:128], parts_ref[:, :, 128:256]
    largest = right[:, :, 0:1]
    top = jnp.max(largest, axis=0, keepdims=True)
    scaled = jnp.exp(largest - top)
    lane = lax.broadcasted_iota(jnp.int32, (1, 8, 128), 2)
    sums = jnp.sum(left * scaled, axis=0, keepdims=True)
    label_rows = jnp.sum(left, axis=0, keepdims=True)
    totals = jnp.sum(right[:, :, 1:2] * scaled, axis=0, keepdims=True)
    left = jnp.where(lane < 64, sums, label_rows)
    right = jnp.where(lane == 0, top, jnp.where(lane == 1, totals, 0.0))
    out_ref[:, :, 0:128] = jnp.broadcast_to(left, (32, 8, 128))
    out_ref[:, :, 128:256] = jnp.broadcast_to(right, (32, 8, 128))


def end_kernel(half_ref, parts_ref, mapped_ref, even_ref, odd_ref, right_ref, queries_ref, out_ref):
    def precise(first, second):
        return jnp.dot(first, second, precision=PRECISE, preferred_element_type=jnp.float32)

    parts = [parts_ref[:, part].reshape(64, 256) for part in range(4)]
    largest = [part[:, 128:129] for part in parts]
    top = functools.reduce(jnp.maximum, largest)
    scaled = [jnp.exp(value - top) for value in largest]
    totals = sum(part[:, 129:130] * scale for part, scale in zip(parts, scaled))
    sums = sum(part[:, 0:64] * scale for part, scale in zip(parts, scaled))
    projected = sums / totals - sum(part[:, 64:128] for part in parts)
    feature = precise(mapped_ref[...], projected)
    even = precise(precise(even_ref[...], feature), right_ref[...])
    odd = precise(precise(odd_ref[...], feature), right_ref[...])
    flat = jnp.concatenate([even, odd], axis=1)
    products = jnp.zeros((128, 128), jnp.float32)
    for pair in range(32):
        products += queries_ref[:, 128 * pair : 128 * pair + 128] * flat[pair : pair + 1, :]
    lane = lax.broadcasted_iota(jnp.int32, (8, 16), 1)
    scores = jnp.zeros((8, 16), jnp.float32)
    for block in range(16):
        group = block // 2 * 2 + jnp.where(half_ref[0] == 0, block % 2, 1 - block % 2)
        column = jnp.sum(products[8 * block : 8 * block + 8], axis=1, keepdims=True)
        scores = jnp.where(lane == group, column, scores)
    out_ref[...] = scores


def product_specs():
    rows = pl.BlockSpec((ROWS, DEPTH), lambda step, where: (0, step))
    weight = pl.BlockSpec((DEPTH, 256), lambda step, where: (where[0] * STEPS + step, 0))
    return [rows, rows] + [weight] * 4


def whole(shape):
    return pl.BlockSpec(shape, lambda step, where: (0,) * len(shape))


COST = dict(flops=2 * 256 * 2304 * 1024, bytes_accessed=7_000_000)


def first_products(where, near, far, weights):
    return pl.pallas_call(
        first_kernel,
        out_shape=jax.ShapeDtypeStruct((256, 1024), jnp.float32),
        grid_spec=pltpu.PrefetchScalarGridSpec(
            num_scalar_prefetch=1,
            grid=(STEPS,),
            in_specs=product_specs(),
            out_specs=whole((256, 1024)),
        ),
        compiler_params=pltpu.CompilerParams(vmem_limit_bytes=24 << 20),
        cost_estimate=pl.CostEstimate(transcendentals=0, **COST),
    )(where, near, far, *weights)


def last_products(where, near, far, weights, begun, table, label_rows):
    return pl.pallas_call(
        last_kernel,
        out_shape=jax.ShapeDtypeStruct((4, 2, 32, 256), jnp.float32),
        grid_spec=pltpu.PrefetchScalarGridSpec(
            num_scalar_prefetch=1,
            grid=(STEPS,),
            in_specs=product_specs() + [whole((256, 1024)), whole((1024, 64)), whole((256, 64))],
            out_specs=whole((4, 2, 32, 256)),
            scratch_shapes=[pltpu.VMEM((256, 1024), jnp.float32)],
        ),
        compiler_params=pltpu.CompilerParams(vmem_limit_bytes=24 << 20),
        cost_estimate=pl.CostEstimate(transcendentals=256 * 1024, **COST),
    )(where, near, far, *weights, begun, table, label_rows)


def local(hidden, labels, unembed, in_proj, out_proj, left_inv, right_inv, queries):
    core, xl, xh, zl = [lax.axis_index(name) for name in ("core", "xl", "xh", "zl")]
    y = lax.axis_index("yh") * 2 + lax.axis_index("yl")
    rows = 16 * (2 * lax.axis_index("yl") + core)
    z = lax.axis_index("zh") * 2 + zl

    chosen = lax.dynamic_slice(hidden, (rows, 2304 * xl), (16, 2304))
    picked = lax.dynamic_slice(labels, (rows,), (16,))
    digits = jnp.stack([picked // 65536, (picked // 256) % 256, picked % 256], axis=1)
    digits = jnp.pad(digits, ((0, 0), (0, 125))).astype(jnp.bfloat16)
    chosen = jnp.concatenate([chosen, digits], axis=1)
    near = spread_out(chosen, ("zh", "xh"), 8).reshape(ROWS, 2432)
    far = both_ways(near, ("zh", "zl"), 8)
    near_x = both_ways(near, ("xh", "xl"), 4)
    far_x = both_ways(far, ("xh", "xl"), 4)

    late_query, _ = lax.optimization_barrier((queries[0], near))
    query_pair = jnp.stack([late_query, lax.ppermute(late_query, "xh", SWAP)])
    every_query = lax.all_gather(query_pair, ("zh", "zl"), axis=0)

    weights = [unembed, both_ways(unembed, ("yh", "yl"), 8)]
    tables = jnp.concatenate([out_proj, both_ways(out_proj, ("yh", "yl"), 8)], axis=0)
    late_weight, tables, _, _ = lax.optimization_barrier((weights[1], tables, far, near_x))
    weights += [lax.ppermute(block, "core", SWAP) for block in (unembed, late_weight)]
    table = jnp.concatenate([tables, lax.ppermute(tables, "core", SWAP)], axis=0)

    def block_start(at_y, at_core):
        return (((z * 2 + xh) * 2 + xl) * 16 + at_y * 2 + at_core) * 256

    below, above = (y + 7) % 8, (y + 1) % 8
    starts = [
        block_start(y, core),
        block_start(jnp.where(core == 0, below, above), core),
        block_start(y, 1 - core),
        block_start(jnp.where(core == 0, above, below), 1 - core),
    ]
    ids = lax.iota(jnp.int32, 256)
    column_ids = jnp.concatenate([start + ids for start in starts])
    digits = jnp.concatenate([near[:, 2304:], far[:, 2304:]], axis=0).astype(jnp.int32)
    every_label = digits[:, 0:1] * 65536 + digits[:, 1:2] * 256 + digits[:, 2:3]
    mask = (every_label == column_ids[None, :]).astype(jnp.float32)
    label_rows = jnp.dot(mask, table, precision=PRECISE)
    mapped = jnp.dot(hidden, in_proj, preferred_element_type=jnp.float32)

    begun = first_products(jnp.stack([xl, zl]), near, far, weights)
    packed = last_products(jnp.stack([1 - xl, zl]), near_x, far_x, weights, begun, table, label_rows)

    parts = exchange(packed.reshape(32, 8, 256), ("zh", "zl", "xh", "xl"))
    merged = pl.pallas_call(
        merge_kernel,
        out_shape=jax.ShapeDtypeStruct((32, 8, 256), jnp.float32),
        cost_estimate=pl.CostEstimate(flops=300_000, bytes_accessed=600_000, transcendentals=256),
    )(parts)
    parts = exchange(merged, VOC).reshape(2, 4, 4, 8, 256)
    mapped = jnp.transpose(mapped.reshape(4, 2, 8, 64), (3, 1, 0, 2)).reshape(64, 64)
    scores = pl.pallas_call(
        end_kernel,
        out_shape=jax.ShapeDtypeStruct((8, 16), jnp.float32),
        in_specs=[pl.BlockSpec(memory_space=pltpu.SMEM)] + [pl.BlockSpec(memory_space=pltpu.VMEM)] * 6,
        cost_estimate=pl.CostEstimate(flops=2_000_000, bytes_accessed=2_500_000, transcendentals=256),
        compiler_params=pltpu.CompilerParams(vmem_limit_bytes=24 << 20),
    )(xh.reshape(1), parts, mapped, left_inv[0::2], left_inv[1::2], right_inv, every_query.reshape(128, 4096))
    return scores.T[None]


def solution(mesh):
    fine = Mesh(mesh.devices.reshape(4, 2, 2, 2, 4, 2, 2), EVERY)
    in_specs = (
        P(DP, None),
        P(DP),
        P(None, EVERY),
        P(),
        P(EVERY, None),
        P(),
        P(),
        P(DP, VOC, None),
    )
    out_specs = P(DP, None, VOC)
    return jax.shard_map(local, mesh=fine, in_specs=in_specs, out_specs=out_specs, check_vma=False)
```

```python
import functools
import jax
import jax.numpy as jnp
from jax import lax
from jax.experimental import pallas as pl
from jax.experimental.pallas import tpu as pltpu
from jax.sharding import Mesh, PartitionSpec as P

PRECISE = lax.Precision.HIGHEST
EVERY = ("zh", "zl", "xh", "xl", "yh", "yl", "core")
DP = ("zh", "zl", "xh")
VOC = ("xl", "yh", "yl", "core")
SWAP = [(0, 1), (1, 0)]
STEPS = 3
DEPTH = 2304 // STEPS
ROWS = 128


def exchange(blocks, axes):
    return lax.all_to_all(blocks, axes, split_axis=0, concat_axis=0, tiled=True)


def spread_out(block, axes, count):
    return exchange(jnp.broadcast_to(block[None], (count,) + block.shape), axes)


def both_ways(value, axes, count):
    pairs = [(2 * i, 2 * ((i + 1) % count)) for i in range(count)]
    pairs += [(2 * i + 1, 2 * ((i - 1) % count) + 1) for i in range(count)]
    return lax.ppermute(value, axes + ("core",), pairs)


def add_products(near_ref, far_ref, weight_refs, acc_ref):
    for block, weight in enumerate(weight_refs):
        columns = pl.ds(256 * block, 256)
        for start, rows in ((0, near_ref), (ROWS, far_ref)):
            acc_ref[pl.ds(start, ROWS), columns] += jnp.dot(
                rows[...], weight[...], preferred_element_type=jnp.float32
            )


def first_kernel(where_ref, near_ref, far_ref, w0, w1, w2, w3, acc_ref):
    @pl.when(pl.program_id(0) == 0)
    def _():
        acc_ref[...] = jnp.zeros_like(acc_ref)

    add_products(near_ref, far_ref, (w0, w1, w2, w3), acc_ref)


def last_kernel(where_ref, near_ref, far_ref, w0, w1, w2, w3, begun_ref, table_ref, label_ref, out_ref, acc_ref):
    step = pl.program_id(0)

    @pl.when(step == 0)
    def _():
        acc_ref[...] = begun_ref[...]

    add_products(near_ref, far_ref, (w0, w1, w2, w3), acc_ref)

    @pl.when(step == STEPS - 1)
    def _():
        logits = acc_ref[...]
        largest = jnp.max(logits, axis=1, keepdims=True)
        exponent = jnp.exp(logits - largest)
        totals = jnp.sum(exponent, axis=1, keepdims=True)
        sums = jnp.dot(exponent, table_ref[...], precision=PRECISE, preferred_element_type=jnp.float32)
        left = jnp.concatenate([sums, label_ref[...]], axis=1)
        lane = lax.broadcasted_iota(jnp.int32, (2 * ROWS, 128), 1)
        right = jnp.where(lane == 0, largest, jnp.where(lane == 1, totals, 0.0))
        parity = where_ref[1]
        for start, place in ((0, parity), (ROWS, 1 - parity)):
            out_ref[:, pl.ds(place, 1), :, 0:128] = left[start : start + ROWS].reshape(4, 1, 32, 128)
            out_ref[:, pl.ds(place, 1), :, 128:256] = right[start : start + ROWS].reshape(4, 1, 32, 128)


def merge_kernel(parts_ref, out_ref):
    left, right = parts_ref[:, :, 0:128], parts_ref[:, :, 128:256]
    largest = right[:, :, 0:1]
    top = jnp.max(largest, axis=0, keepdims=True)
    scaled = jnp.exp(largest - top)
    lane = lax.broadcasted_iota(jnp.int32, (1, 8, 128), 2)
    sums = jnp.sum(left * scaled, axis=0, keepdims=True)
    label_rows = jnp.sum(left, axis=0, keepdims=True)
    totals = jnp.sum(right[:, :, 1:2] * scaled, axis=0, keepdims=True)
    left = jnp.where(lane < 64, sums, label_rows)
    right = jnp.where(lane == 0, top, jnp.where(lane == 1, totals, 0.0))
    out_ref[:, :, 0:128] = jnp.broadcast_to(left, (32, 8, 128))
    out_ref[:, :, 128:256] = jnp.broadcast_to(right, (32, 8, 128))


def end_kernel(half_ref, parts_ref, mapped_ref, even_ref, odd_ref, right_ref, queries_ref, out_ref):
    def precise(first, second):
        return jnp.dot(first, second, precision=PRECISE, preferred_element_type=jnp.float32)

    parts = [parts_ref[:, part].reshape(64, 256) for part in range(4)]
    largest = [part[:, 128:129] for part in parts]
    top = functools.reduce(jnp.maximum, largest)
    scaled = [jnp.exp(value - top) for value in largest]
    totals = sum(part[:, 129:130] * scale for part, scale in zip(parts, scaled))
    sums = sum(part[:, 0:64] * scale for part, scale in zip(parts, scaled))
    projected = sums / totals - sum(part[:, 64:128] for part in parts)
    feature = precise(mapped_ref[...], projected)
    even = precise(precise(even_ref[...], feature), right_ref[...])
    odd = precise(precise(odd_ref[...], feature), right_ref[...])
    flat = jnp.concatenate([even, odd], axis=1)
    products = jnp.zeros((128, 128), jnp.float32)
    for pair in range(32):
        products += queries_ref[:, 128 * pair : 128 * pair + 128] * flat[pair : pair + 1, :]
    lane = lax.broadcasted_iota(jnp.int32, (8, 16), 1)
    scores = jnp.zeros((8, 16), jnp.float32)
    for block in range(16):
        group = block // 2 * 2 + jnp.where(half_ref[0] == 0, block % 2, 1 - block % 2)
        column = jnp.sum(products[8 * block : 8 * block + 8], axis=1, keepdims=True)
        scores = jnp.where(lane == group, column, scores)
    out_ref[...] = scores


def product_specs():
    rows = pl.BlockSpec((ROWS, DEPTH), lambda step, where: (0, step))
    weight = pl.BlockSpec((DEPTH, 256), lambda step, where: (where[0] * STEPS + step, 0))
    return [rows, rows] + [weight] * 4


def whole(shape):
    return pl.BlockSpec(shape, lambda step, where: (0,) * len(shape))


COST = dict(flops=2 * 256 * 2304 * 1024, bytes_accessed=7_000_000)


def first_products(where, near, far, weights):
    return pl.pallas_call(
        first_kernel,
        out_shape=jax.ShapeDtypeStruct((256, 1024), jnp.float32),
        grid_spec=pltpu.PrefetchScalarGridSpec(
            num_scalar_prefetch=1,
            grid=(STEPS,),
            in_specs=product_specs(),
            out_specs=whole((256, 1024)),
        ),
        compiler_params=pltpu.CompilerParams(vmem_limit_bytes=24 << 20),
        cost_estimate=pl.CostEstimate(transcendentals=0, **COST),
    )(where, near, far, *weights)


def last_products(where, near, far, weights, begun, table, label_rows):
    return pl.pallas_call(
        last_kernel,
        out_shape=jax.ShapeDtypeStruct((4, 2, 32, 256), jnp.float32),
        grid_spec=pltpu.PrefetchScalarGridSpec(
            num_scalar_prefetch=1,
            grid=(STEPS,),
            in_specs=product_specs() + [whole((256, 1024)), whole((1024, 64)), whole((256, 64))],
            out_specs=whole((4, 2, 32, 256)),
            scratch_shapes=[pltpu.VMEM((256, 1024), jnp.float32)],
        ),
        compiler_params=pltpu.CompilerParams(vmem_limit_bytes=24 << 20),
        cost_estimate=pl.CostEstimate(transcendentals=256 * 1024, **COST),
    )(where, near, far, *weights, begun, table, label_rows)


def local(hidden, labels, unembed, in_proj, out_proj, left_inv, right_inv, queries):
    core, xl, xh, zl = [lax.axis_index(name) for name in ("core", "xl", "xh", "zl")]
    y = lax.axis_index("yh") * 2 + lax.axis_index("yl")
    rows = 16 * (2 * lax.axis_index("yl") + core)
    z = lax.axis_index("zh") * 2 + zl

    chosen = lax.dynamic_slice(hidden, (rows, 2304 * xl), (16, 2304))
    picked = lax.dynamic_slice(labels, (rows,), (16,))
    digits = jnp.stack([picked // 65536, (picked // 256) % 256, picked % 256], axis=1)
    digits = jnp.pad(digits, ((0, 0), (0, 125))).astype(jnp.bfloat16)
    chosen = jnp.concatenate([chosen, digits], axis=1)
    near = spread_out(chosen, ("zh", "xh"), 8).reshape(ROWS, 2432)

    swapped = lax.ppermute(unembed, "core", SWAP)
    tables = jnp.concatenate([out_proj, both_ways(out_proj, ("yh", "yl"), 8)], axis=0)
    table = jnp.concatenate([tables, lax.ppermute(tables, "core", SWAP)], axis=0)
    query_pair = jnp.stack([queries[0], lax.ppermute(queries[0], "xh", SWAP)])
    near, swapped, table, query_pair = lax.optimization_barrier((near, swapped, table, query_pair))

    far = both_ways(near, ("zh", "zl"), 8)
    near_x = both_ways(near, ("xh", "xl"), 4)
    far_x = both_ways(far, ("xh", "xl"), 4)
    every_query = lax.all_gather(query_pair, ("zh", "zl"), axis=0)

    moved = both_ways(unembed, ("yh", "yl"), 8)
    late, _, _ = lax.optimization_barrier((moved, far, near_x))
    weights = [unembed, moved, swapped, lax.ppermute(late, "core", SWAP)]

    def block_start(at_y, at_core):
        return (((z * 2 + xh) * 2 + xl) * 16 + at_y * 2 + at_core) * 256

    below, above = (y + 7) % 8, (y + 1) % 8
    starts = [
        block_start(y, core),
        block_start(jnp.where(core == 0, below, above), core),
        block_start(y, 1 - core),
        block_start(jnp.where(core == 0, above, below), 1 - core),
    ]
    ids = lax.iota(jnp.int32, 256)
    column_ids = jnp.concatenate([start + ids for start in starts])
    digits = jnp.concatenate([near[:, 2304:], far[:, 2304:]], axis=0).astype(jnp.int32)
    every_label = digits[:, 0:1] * 65536 + digits[:, 1:2] * 256 + digits[:, 2:3]
    mask = (every_label == column_ids[None, :]).astype(jnp.float32)
    label_rows = jnp.dot(mask, table, precision=PRECISE)
    mapped = jnp.dot(hidden, in_proj, preferred_element_type=jnp.float32)

    begun = first_products(jnp.stack([xl, zl]), near, far, weights)
    packed = last_products(jnp.stack([1 - xl, zl]), near_x, far_x, weights, begun, table, label_rows)

    parts = exchange(packed.reshape(32, 8, 256), ("zh", "zl", "xh", "xl"))
    parts, every_query = lax.optimization_barrier((parts, every_query))
    merged = pl.pallas_call(
        merge_kernel,
        out_shape=jax.ShapeDtypeStruct((32, 8, 256), jnp.float32),
        cost_estimate=pl.CostEstimate(flops=300_000, bytes_accessed=600_000, transcendentals=256),
    )(parts)
    parts = exchange(merged, VOC).reshape(2, 4, 4, 8, 256)
    mapped = jnp.transpose(mapped.reshape(4, 2, 8, 64), (3, 1, 0, 2)).reshape(64, 64)
    scores = pl.pallas_call(
        end_kernel,
        out_shape=jax.ShapeDtypeStruct((8, 16), jnp.float32),
        in_specs=[pl.BlockSpec(memory_space=pltpu.SMEM)] + [pl.BlockSpec(memory_space=pltpu.VMEM)] * 6,
        cost_estimate=pl.CostEstimate(flops=2_000_000, bytes_accessed=2_500_000, transcendentals=256),
        compiler_params=pltpu.CompilerParams(vmem_limit_bytes=24 << 20),
    )(xh.reshape(1), parts, mapped, left_inv[0::2], left_inv[1::2], right_inv, every_query.reshape(128, 4096))
    return scores.T[None]


def solution(mesh):
    fine = Mesh(mesh.devices.reshape(4, 2, 2, 2, 4, 2, 2), EVERY)
    in_specs = (
        P(DP, None),
        P(DP),
        P(None, EVERY),
        P(),
        P(EVERY, None),
        P(),
        P(),
        P(DP, VOC, None),
    )
    out_specs = P(DP, None, VOC)
    return jax.shard_map(local, mesh=fine, in_specs=in_specs, out_specs=out_specs, check_vma=False)
```

```python
import functools
import jax
import jax.numpy as jnp
from jax import lax
from jax.experimental import pallas as pl
from jax.experimental.pallas import tpu as pltpu
from jax.sharding import Mesh, PartitionSpec as P

PRECISE = lax.Precision.HIGHEST
EVERY = ("zh", "zl", "xh", "xl", "yh", "yl", "core")
DP = ("zh", "zl", "xh")
VOC = ("xl", "yh", "yl", "core")
SWAP = [(0, 1), (1, 0)]
STEPS = 3
DEPTH = 2304 // STEPS
ROWS = 128


def exchange(blocks, axes):
    return lax.all_to_all(blocks, axes, split_axis=0, concat_axis=0, tiled=True)


def spread_out(block, axes, count):
    return exchange(jnp.broadcast_to(block[None], (count,) + block.shape), axes)


def both_ways(value, axes, count):
    pairs = [(2 * i, 2 * ((i + 1) % count)) for i in range(count)]
    pairs += [(2 * i + 1, 2 * ((i - 1) % count) + 1) for i in range(count)]
    return lax.ppermute(value, axes + ("core",), pairs)


def diagonal(value):
    pairs = []
    for z in range(8):
        for x in range(4):
            for core, by in ((0, 1), (1, -1)):
                to = (z + by) % 8 * 4 + (x + by) % 4
                pairs.append(((z * 4 + x) * 2 + core, to * 2 + core))
    return lax.ppermute(value, ("zh", "zl", "xh", "xl", "core"), pairs)


def add_products(near_ref, far_ref, weight_refs, acc_ref, first_column=0):
    for block, weight in enumerate(weight_refs):
        columns = pl.ds(first_column + 256 * block, 256)
        for start, rows in ((0, near_ref), (ROWS, far_ref)):
            acc_ref[pl.ds(start, ROWS), columns] += jnp.dot(
                rows[...], weight[...], preferred_element_type=jnp.float32
            )


def times_block(values, block_ref):
    parts = block_ref[...].astype(jnp.float32)
    table = parts[0:64] + parts[64:128] + parts[128:192]
    return lax.dot_general(
        values, table, (((1,), (1,)), ((), ())), precision=PRECISE, preferred_element_type=jnp.float32
    )


def label_rows_of(near_digits, far_digits, starts, tables):
    digits = jnp.concatenate([near_digits[...], far_digits[...]], axis=0).astype(jnp.float32)
    labels = digits[:, 0:1] * 65536.0 + digits[:, 1:2] * 256.0 + digits[:, 2:3]
    ids = lax.broadcasted_iota(jnp.int32, (2 * ROWS, 256), 1)
    rows = jnp.zeros((2 * ROWS, 64), jnp.float32)
    for start, table in zip(starts, tables):
        columns = (ids + start).astype(jnp.float32)
        rows += times_block(jnp.where(labels == columns, 1.0, 0.0), table)
    return rows


def first_kernel(where_ref, near_ref, far_ref, w0, w1, w2, near_digits, far_digits, t0, t1, t2, acc_ref, label_ref):
    @pl.when(pl.program_id(0) == 0)
    def _():
        acc_ref[...] = jnp.zeros_like(acc_ref)
        label_ref[...] = label_rows_of(near_digits, far_digits, [where_ref[3 + i] for i in range(3)], (t0, t1, t2))

    add_products(near_ref, far_ref, (w0, w1, w2), acc_ref)


def last_kernel(
    where_ref, near_ref, far_ref, w0, w1, w2, w3, near3_ref, far3_ref, own3_ref, near_digits, far_digits, t0, t1, t2, t3, begun_ref, label_ref, out_ref, acc_ref
):
    step = pl.program_id(0)

    @pl.when(step == 0)
    def _():
        acc_ref[:, 0:768] = begun_ref[...]
        acc_ref[:, 768:1024] = jnp.zeros((2 * ROWS, 256), jnp.float32)

    add_products(near_ref, far_ref, (w0, w1, w2, w3), acc_ref)
    add_products(near3_ref, far3_ref, (own3_ref,), acc_ref, 768)

    @pl.when(step == STEPS - 1)
    def _():
        logits = acc_ref[...]
        largest = jnp.max(logits, axis=1, keepdims=True)
        exponent = jnp.exp(logits - largest)
        totals = jnp.sum(exponent, axis=1, keepdims=True)
        sums = jnp.zeros((2 * ROWS, 64), jnp.float32)
        for block, table in enumerate((t0, t1, t2, t3)):
            sums += times_block(exponent[:, 256 * block : 256 * block + 256], table)
        label_rows = label_ref[...] + label_rows_of(near_digits, far_digits, [where_ref[6]], [t3])
        left = jnp.concatenate([sums, label_rows], axis=1)
        lane = lax.broadcasted_iota(jnp.int32, (2 * ROWS, 128), 1)
        right = jnp.where(lane == 0, largest, jnp.where(lane == 1, totals, 0.0))
        parity = where_ref[1]
        for start, place in ((0, parity), (ROWS, 1 - parity)):
            out_ref[:, pl.ds(place, 1), :, 0:128] = left[start : start + ROWS].reshape(4, 1, 32, 128)
            out_ref[:, pl.ds(place, 1), :, 128:256] = right[start : start + ROWS].reshape(4, 1, 32, 128)


def merge_kernel(parts_ref, out_ref):
    left, right = parts_ref[:, :, 0:128], parts_ref[:, :, 128:256]
    largest = right[:, :, 0:1]
    top = jnp.max(largest, axis=0, keepdims=True)
    scaled = jnp.exp(largest - top)
    lane = lax.broadcasted_iota(jnp.int32, (1, 8, 128), 2)
    sums = jnp.sum(left * scaled, axis=0, keepdims=True)
    label_rows = jnp.sum(left, axis=0, keepdims=True)
    totals = jnp.sum(right[:, :, 1:2] * scaled, axis=0, keepdims=True)
    left = jnp.where(lane < 64, sums, label_rows)
    right = jnp.where(lane == 0, top, jnp.where(lane == 1, totals, 0.0))
    out_ref[:, :, 0:128] = jnp.broadcast_to(left, (32, 8, 128))
    out_ref[:, :, 128:256] = jnp.broadcast_to(right, (32, 8, 128))


def end_kernel(parts_ref, mapped_ref, even_ref, odd_ref, right_ref, queries_ref, out_ref):
    def precise(first, second):
        return jnp.dot(first, second, precision=PRECISE, preferred_element_type=jnp.float32)

    parts = [parts_ref[:, part].reshape(64, 256) for part in range(4)]
    largest = [part[:, 128:129] for part in parts]
    top = functools.reduce(jnp.maximum, largest)
    scaled = [jnp.exp(value - top) for value in largest]
    totals = sum(part[:, 129:130] * scale for part, scale in zip(parts, scaled))
    sums = sum(part[:, 0:64] * scale for part, scale in zip(parts, scaled))
    projected = sums / totals - sum(part[:, 64:128] for part in parts)
    feature = precise(mapped_ref[...], projected)
    even = precise(precise(even_ref[...], feature), right_ref[...])
    odd = precise(precise(odd_ref[...], feature), right_ref[...])
    flat = jnp.concatenate([even, odd], axis=1)
    products = jnp.zeros((128, 128), jnp.float32)
    for pair in range(32):
        products += queries_ref[:, 128 * pair : 128 * pair + 128] * flat[pair : pair + 1, :]
    lane = lax.broadcasted_iota(jnp.int32, (8, 16), 1)
    scores = jnp.zeros((8, 16), jnp.float32)
    for block in range(16):
        column = jnp.sum(products[8 * block : 8 * block + 8], axis=1, keepdims=True)
        scores = jnp.where(lane == block, column, scores)
    out_ref[...] = scores


def product_specs(blocks, half=0):
    rows = pl.BlockSpec((ROWS, DEPTH), lambda step, where: (0, step))
    weight = pl.BlockSpec((DEPTH, 256), lambda step, where: (where[half] * STEPS + step, 0))
    return [rows, rows] + [weight] * blocks


def side_specs(blocks):
    digits = pl.BlockSpec((ROWS, 128), lambda step, where: (0, 18))
    table = pl.BlockSpec((192, 256), lambda step, where: (24, 0))
    return [digits, digits] + [table] * blocks


def whole(shape):
    return pl.BlockSpec(shape, lambda step, where: (0,) * len(shape))


COST = dict(flops=2 * 256 * 2304 * 1024, bytes_accessed=7_000_000)


def first_products(where, near, far, weights):
    return pl.pallas_call(
        first_kernel,
        out_shape=(jax.ShapeDtypeStruct((256, 768), jnp.float32), jax.ShapeDtypeStruct((256, 64), jnp.float32)),
        grid_spec=pltpu.PrefetchScalarGridSpec(
            num_scalar_prefetch=1,
            grid=(STEPS,),
            in_specs=product_specs(3, 2) + side_specs(3),
            out_specs=(whole((256, 768)), whole((256, 64))),
        ),
        compiler_params=pltpu.CompilerParams(vmem_limit_bytes=24 << 20),
        cost_estimate=pl.CostEstimate(transcendentals=0, **COST),
    )(where, near, far, *weights, near, far, *weights)


def last_products(where, near_x, far_x, weights, near, far, begun, label_rows):
    return pl.pallas_call(
        last_kernel,
        out_shape=jax.ShapeDtypeStruct((4, 2, 32, 256), jnp.float32),
        grid_spec=pltpu.PrefetchScalarGridSpec(
            num_scalar_prefetch=1,
            grid=(STEPS,),
            in_specs=product_specs(4)
            + product_specs(1, 2)
            + side_specs(4)
            + [whole((256, 768)), whole((256, 64))],
            out_specs=whole((4, 2, 32, 256)),
            scratch_shapes=[pltpu.VMEM((256, 1024), jnp.float32)],
        ),
        compiler_params=pltpu.CompilerParams(vmem_limit_bytes=24 << 20),
        cost_estimate=pl.CostEstimate(transcendentals=256 * 1024, **COST),
    )(where, near_x, far_x, *weights, near, far, weights[3], near, far, *weights, begun, label_rows)


def local(hidden, labels, unembed, in_proj, out_proj, left_inv, right_inv, queries):
    core, xl, xh, zl = [lax.axis_index(name) for name in ("core", "xl", "xh", "zl")]
    y = lax.axis_index("yh") * 2 + lax.axis_index("yl")
    rows = 16 * (2 * lax.axis_index("yl") + core)
    z = lax.axis_index("zh") * 2 + zl

    chosen = lax.dynamic_slice(hidden, (rows, 2304 * xl), (16, 2304))
    picked = lax.dynamic_slice(labels, (rows,), (16,))
    digits = jnp.stack([picked // 65536, (picked // 256) % 256, picked % 256], axis=1)
    digits = jnp.pad(digits, ((0, 0), (0, 125))).astype(jnp.bfloat16)
    chosen = jnp.concatenate([chosen, digits], axis=1)
    near = spread_out(chosen, ("zh", "xh"), 8).reshape(ROWS, 2432)

    table = out_proj.T
    high = lax.reduce_precision(table, 8, 7)
    middle = lax.reduce_precision(table - high, 8, 7)
    parts = [part.astype(jnp.bfloat16) for part in (high, middle, table - high - middle)]
    block = jnp.concatenate([unembed] + parts, axis=0)

    query_pair = lax.all_gather(queries[0], "xh", axis=0)
    near, query_pair = lax.optimization_barrier((near, query_pair))
    far = both_ways(near, ("zh", "zl"), 8)
    near_x = both_ways(near, ("xh", "xl"), 4)
    far_x = diagonal(near)
    moved = both_ways(block, ("yh", "yl"), 8)
    every_query = lax.all_gather(query_pair, ("zh", "zl"), axis=0)
    swapped = lax.ppermute(block, "core", SWAP)
    late, _, _ = lax.optimization_barrier((moved, far, near_x))
    weights = [block, moved, swapped, lax.ppermute(late, "core", SWAP)]

    below, above = ((y + 7) % 8) * 2, ((y + 1) % 8) * 2 + 1
    places = [
        2 * y + core,
        jnp.where(core == 0, below, above),
        2 * y + 1 - core,
        jnp.where(core == 0, above, below),
    ]
    starts = [(((z * 2 + xh) * 2 + xl) * 16 + place) * 256 for place in places]
    where = jnp.stack([1 - xl, zl, xl] + starts)
    mapped = jnp.dot(hidden, in_proj, preferred_element_type=jnp.float32)

    begun, label_rows = first_products(where, near, far, weights[:3])
    packed = last_products(where, near_x, far_x, weights, near, far, begun, label_rows)
    parts = exchange(packed.reshape(32, 8, 256), ("zh", "zl", "xh", "xl"))
    merged = pl.pallas_call(
        merge_kernel,
        out_shape=jax.ShapeDtypeStruct((32, 8, 256), jnp.float32),
        cost_estimate=pl.CostEstimate(flops=300_000, bytes_accessed=600_000, transcendentals=256),
    )(parts)
    parts = exchange(merged, VOC).reshape(2, 4, 4, 8, 256)
    mapped = jnp.transpose(mapped.reshape(4, 2, 8, 64), (3, 1, 0, 2)).reshape(64, 64)
    scores = pl.pallas_call(
        end_kernel,
        out_shape=jax.ShapeDtypeStruct((8, 16), jnp.float32),
        in_specs=[pl.BlockSpec(memory_space=pltpu.VMEM)] * 6,
        cost_estimate=pl.CostEstimate(flops=2_000_000, bytes_accessed=2_500_000, transcendentals=256),
        compiler_params=pltpu.CompilerParams(vmem_limit_bytes=24 << 20),
    )(parts, mapped, left_inv[0::2], left_inv[1::2], right_inv, every_query.reshape(128, 4096))
    return scores.T[None]


def solution(mesh):
    fine = Mesh(mesh.devices.reshape(4, 2, 2, 2, 4, 2, 2), EVERY)
    in_specs = (
        P(DP, None),
        P(DP),
        P(None, EVERY),
        P(),
        P(EVERY, None),
        P(),
        P(),
        P(DP, VOC, None),
    )
    out_specs = P(DP, None, VOC)
    return jax.shard_map(local, mesh=fine, in_specs=in_specs, out_specs=out_specs, check_vma=False)
```

```python
import functools
import jax
import jax.numpy as jnp
from jax import lax
from jax.experimental import pallas as pl
from jax.experimental.pallas import tpu as pltpu
from jax.sharding import Mesh, PartitionSpec as P

PRECISE = lax.Precision.HIGHEST
EVERY = ("zh", "zl", "xh", "xl", "yh", "yl", "core")
DP = ("zh", "zl", "xh")
VOC = ("xl", "yh", "yl", "core")
SWAP = [(0, 1), (1, 0)]
STEPS = 3
DEPTH = 2304 // STEPS
ROWS = 128


def exchange(blocks, axes):
    return lax.all_to_all(blocks, axes, split_axis=0, concat_axis=0, tiled=True)


def spread_out(block, axes, count):
    return exchange(jnp.broadcast_to(block[None], (count,) + block.shape), axes)


def both_ways(value, axes, count):
    pairs = [(2 * i, 2 * ((i + 1) % count)) for i in range(count)]
    pairs += [(2 * i + 1, 2 * ((i - 1) % count) + 1) for i in range(count)]
    return lax.ppermute(value, axes + ("core",), pairs)


def add_products(near_ref, far_ref, weight_refs, acc_ref, first_column=0):
    for block, weight in enumerate(weight_refs):
        columns = pl.ds(first_column + 256 * block, 256)
        for start, rows in ((0, near_ref), (ROWS, far_ref)):
            acc_ref[pl.ds(start, ROWS), columns] += jnp.dot(
                rows[...], weight[...], preferred_element_type=jnp.float32
            )


def times_block(values, block_ref):
    parts = block_ref[...].astype(jnp.float32)
    table = parts[0:64] + parts[64:128] + parts[128:192]
    return lax.dot_general(
        values, table, (((1,), (1,)), ((), ())), precision=PRECISE, preferred_element_type=jnp.float32
    )


def label_rows_of(near_digits, far_digits, starts, tables):
    digits = jnp.concatenate([near_digits[...], far_digits[...]], axis=0).astype(jnp.float32)
    labels = digits[:, 0:1] * 65536.0 + digits[:, 1:2] * 256.0 + digits[:, 2:3]
    ids = lax.broadcasted_iota(jnp.int32, (2 * ROWS, 256), 1)
    rows = jnp.zeros((2 * ROWS, 64), jnp.float32)
    for start, table in zip(starts, tables):
        columns = (ids + start).astype(jnp.float32)
        rows += times_block(jnp.where(labels == columns, 1.0, 0.0), table)
    return rows


def first_kernel(where_ref, near_ref, far_ref, w0, w1, w2, near_digits, far_digits, t0, t1, t2, acc_ref, label_ref):
    @pl.when(pl.program_id(0) == 0)
    def _():
        acc_ref[...] = jnp.zeros_like(acc_ref)
        label_ref[...] = label_rows_of(near_digits, far_digits, [where_ref[3 + i] for i in range(3)], (t0, t1, t2))

    add_products(near_ref, far_ref, (w0, w1, w2), acc_ref)


def last_kernel(
    where_ref, near_ref, far_ref, w0, w1, w2, w3, near3_ref, far3_ref, own3_ref, near_digits, far_digits, t0, t1, t2, t3, begun_ref, label_ref, out_ref, acc_ref
):
    step = pl.program_id(0)

    @pl.when(step == 0)
    def _():
        acc_ref[:, 0:768] = begun_ref[...]
        acc_ref[:, 768:1024] = jnp.zeros((2 * ROWS, 256), jnp.float32)

    add_products(near_ref, far_ref, (w0, w1, w2, w3), acc_ref)
    add_products(near3_ref, far3_ref, (own3_ref,), acc_ref, 768)

    @pl.when(step == STEPS - 1)
    def _():
        logits = acc_ref[...]
        largest = jnp.max(logits, axis=1, keepdims=True)
        exponent = jnp.exp(logits - largest)
        totals = jnp.sum(exponent, axis=1, keepdims=True)
        sums = jnp.zeros((2 * ROWS, 64), jnp.float32)
        for block, table in enumerate((t0, t1, t2, t3)):
            sums += times_block(exponent[:, 256 * block : 256 * block + 256], table)
        label_rows = label_ref[...] + label_rows_of(near_digits, far_digits, [where_ref[6]], [t3])
        left = jnp.concatenate([sums, label_rows], axis=1)
        lane = lax.broadcasted_iota(jnp.int32, (2 * ROWS, 128), 1)
        right = jnp.where(lane == 0, largest, jnp.where(lane == 1, totals, 0.0))
        parity = where_ref[1]
        for start, place in ((0, parity), (ROWS, 1 - parity)):
            out_ref[:, pl.ds(place, 1), :, 0:128] = left[start : start + ROWS].reshape(4, 1, 32, 128)
            out_ref[:, pl.ds(place, 1), :, 128:256] = right[start : start + ROWS].reshape(4, 1, 32, 128)


def merge_kernel(parts_ref, out_ref):
    left, right = parts_ref[:, :, 0:128], parts_ref[:, :, 128:256]
    largest = right[:, :, 0:1]
    top = jnp.max(largest, axis=0, keepdims=True)
    scaled = jnp.exp(largest - top)
    lane = lax.broadcasted_iota(jnp.int32, (1, 8, 128), 2)
    sums = jnp.sum(left * scaled, axis=0, keepdims=True)
    label_rows = jnp.sum(left, axis=0, keepdims=True)
    totals = jnp.sum(right[:, :, 1:2] * scaled, axis=0, keepdims=True)
    left = jnp.where(lane < 64, sums, label_rows)
    right = jnp.where(lane == 0, top, jnp.where(lane == 1, totals, 0.0))
    out_ref[:, :, 0:128] = jnp.broadcast_to(left, (32, 8, 128))
    out_ref[:, :, 128:256] = jnp.broadcast_to(right, (32, 8, 128))


def end_kernel(parts_ref, mapped_ref, even_ref, odd_ref, right_ref, queries_ref, out_ref):
    def precise(first, second):
        return jnp.dot(first, second, precision=PRECISE, preferred_element_type=jnp.float32)

    parts = [parts_ref[:, part].reshape(64, 256) for part in range(4)]
    largest = [part[:, 128:129] for part in parts]
    top = functools.reduce(jnp.maximum, largest)
    scaled = [jnp.exp(value - top) for value in largest]
    totals = sum(part[:, 129:130] * scale for part, scale in zip(parts, scaled))
    sums = sum(part[:, 0:64] * scale for part, scale in zip(parts, scaled))
    projected = sums / totals - sum(part[:, 64:128] for part in parts)
    feature = precise(mapped_ref[...], projected)
    even = precise(precise(even_ref[...], feature), right_ref[...])
    odd = precise(precise(odd_ref[...], feature), right_ref[...])
    flat = jnp.concatenate([even, odd], axis=1)
    products = jnp.zeros((128, 128), jnp.float32)
    for pair in range(32):
        products += queries_ref[:, 128 * pair : 128 * pair + 128] * flat[pair : pair + 1, :]
    lane = lax.broadcasted_iota(jnp.int32, (8, 16), 1)
    scores = jnp.zeros((8, 16), jnp.float32)
    for block in range(16):
        column = jnp.sum(products[8 * block : 8 * block + 8], axis=1, keepdims=True)
        scores = jnp.where(lane == block, column, scores)
    out_ref[...] = scores


def product_specs(blocks, half=0):
    rows = pl.BlockSpec((ROWS, DEPTH), lambda step, where: (0, step))
    weight = pl.BlockSpec((DEPTH, 256), lambda step, where: (where[half] * STEPS + step, 0))
    return [rows, rows] + [weight] * blocks


def side_specs(blocks):
    digits = pl.BlockSpec((ROWS, 128), lambda step, where: (0, 18))
    table = pl.BlockSpec((192, 256), lambda step, where: (24, 0))
    return [digits, digits] + [table] * blocks


def whole(shape):
    return pl.BlockSpec(shape, lambda step, where: (0,) * len(shape))


COST = dict(flops=2 * 256 * 2304 * 1024, bytes_accessed=7_000_000)


def first_products(where, near, far, weights):
    return pl.pallas_call(
        first_kernel,
        out_shape=(jax.ShapeDtypeStruct((256, 768), jnp.float32), jax.ShapeDtypeStruct((256, 64), jnp.float32)),
        grid_spec=pltpu.PrefetchScalarGridSpec(
            num_scalar_prefetch=1,
            grid=(STEPS,),
            in_specs=product_specs(3, 2) + side_specs(3),
            out_specs=(whole((256, 768)), whole((256, 64))),
        ),
        compiler_params=pltpu.CompilerParams(vmem_limit_bytes=24 << 20),
        cost_estimate=pl.CostEstimate(transcendentals=0, **COST),
    )(where, near, far, *weights, near, far, *weights)


def last_products(where, near_x, far_x, weights, near, far, begun, label_rows):
    return pl.pallas_call(
        last_kernel,
        out_shape=jax.ShapeDtypeStruct((4, 2, 32, 256), jnp.float32),
        grid_spec=pltpu.PrefetchScalarGridSpec(
            num_scalar_prefetch=1,
            grid=(STEPS,),
            in_specs=product_specs(4)
            + product_specs(1, 2)
            + side_specs(4)
            + [whole((256, 768)), whole((256, 64))],
            out_specs=whole((4, 2, 32, 256)),
            scratch_shapes=[pltpu.VMEM((256, 1024), jnp.float32)],
        ),
        compiler_params=pltpu.CompilerParams(vmem_limit_bytes=24 << 20),
        cost_estimate=pl.CostEstimate(transcendentals=256 * 1024, **COST),
    )(where, near_x, far_x, *weights, near, far, weights[3], near, far, *weights, begun, label_rows)


def local(hidden, labels, unembed, in_proj, out_proj, left_inv, right_inv, queries):
    core, xl, xh, zl = [lax.axis_index(name) for name in ("core", "xl", "xh", "zl")]
    y = lax.axis_index("yh") * 2 + lax.axis_index("yl")
    rows = 16 * (2 * lax.axis_index("yl") + core)
    z = lax.axis_index("zh") * 2 + zl

    chosen = lax.dynamic_slice(hidden, (rows, 2304 * xl), (16, 2304))
    picked = lax.dynamic_slice(labels, (rows,), (16,))
    digits = jnp.stack([picked // 65536, (picked // 256) % 256, picked % 256], axis=1)
    digits = jnp.pad(digits, ((0, 0), (0, 125))).astype(jnp.bfloat16)
    chosen = jnp.concatenate([chosen, digits], axis=1)
    near = spread_out(chosen, ("zh", "xh"), 8).reshape(ROWS, 2432)

    table = out_proj.T
    high = lax.reduce_precision(table, 8, 7)
    middle = lax.reduce_precision(table - high, 8, 7)
    parts = [part.astype(jnp.bfloat16) for part in (high, middle, table - high - middle)]
    block = jnp.concatenate([unembed] + parts, axis=0)

    query_pair = lax.all_gather(queries[0], "xh", axis=0)
    near, query_pair = lax.optimization_barrier((near, query_pair))
    far = both_ways(near, ("zh", "zl"), 8)
    near_x = both_ways(near, ("xh", "xl"), 4)
    far_x = both_ways(far, ("xh", "xl"), 4)
    moved = both_ways(block, ("yh", "yl"), 8)
    every_query = lax.all_gather(query_pair, ("zh", "zl"), axis=0)
    swapped = lax.ppermute(block, "core", SWAP)
    late, _ = lax.optimization_barrier((moved, far))
    weights = [block, moved, swapped, lax.ppermute(late, "core", SWAP)]

    below, above = ((y + 7) % 8) * 2, ((y + 1) % 8) * 2 + 1
    places = [
        2 * y + core,
        jnp.where(core == 0, below, above),
        2 * y + 1 - core,
        jnp.where(core == 0, above, below),
    ]
    starts = [(((z * 2 + xh) * 2 + xl) * 16 + place) * 256 for place in places]
    where = jnp.stack([1 - xl, zl, xl] + starts)
    mapped = jnp.dot(hidden, in_proj, preferred_element_type=jnp.float32)

    begun, label_rows = first_products(where, near, far, weights[:3])
    packed = last_products(where, near_x, far_x, weights, near, far, begun, label_rows)
    parts = exchange(packed.reshape(32, 8, 256), ("zh", "zl", "xh", "xl"))
    merged = pl.pallas_call(
        merge_kernel,
        out_shape=jax.ShapeDtypeStruct((32, 8, 256), jnp.float32),
        cost_estimate=pl.CostEstimate(flops=300_000, bytes_accessed=600_000, transcendentals=256),
    )(parts)
    merged, every_query = lax.optimization_barrier((merged, every_query))
    parts = exchange(merged, VOC).reshape(2, 4, 4, 8, 256)
    mapped = jnp.transpose(mapped.reshape(4, 2, 8, 64), (3, 1, 0, 2)).reshape(64, 64)
    scores = pl.pallas_call(
        end_kernel,
        out_shape=jax.ShapeDtypeStruct((8, 16), jnp.float32),
        in_specs=[pl.BlockSpec(memory_space=pltpu.VMEM)] * 6,
        cost_estimate=pl.CostEstimate(flops=2_000_000, bytes_accessed=2_500_000, transcendentals=256),
        compiler_params=pltpu.CompilerParams(vmem_limit_bytes=24 << 20),
    )(parts, mapped, left_inv[0::2], left_inv[1::2], right_inv, every_query.reshape(128, 4096))
    return scores.T[None]


def solution(mesh):
    fine = Mesh(mesh.devices.reshape(4, 2, 2, 2, 4, 2, 2), EVERY)
    in_specs = (
        P(DP, None),
        P(DP),
        P(None, EVERY),
        P(),
        P(EVERY, None),
        P(),
        P(),
        P(DP, VOC, None),
    )
    out_specs = P(DP, None, VOC)
    return jax.shard_map(local, mesh=fine, in_specs=in_specs, out_specs=out_specs, check_vma=False)
```

```python
import functools
import jax
import jax.numpy as jnp
from jax import lax
from jax.experimental import pallas as pl
from jax.experimental.pallas import tpu as pltpu
from jax.sharding import Mesh, PartitionSpec as P

PRECISE = lax.Precision.HIGHEST
EVERY = ("zh", "zl", "xh", "xl", "yh", "yl", "core")
DP = ("zh", "zl", "xh")
VOC = ("xl", "yh", "yl", "core")
SWAP = [(0, 1), (1, 0)]
STEPS = 3
DEPTH = 2304 // STEPS
ROWS = 128


def exchange(blocks, axes):
    return lax.all_to_all(blocks, axes, split_axis=0, concat_axis=0, tiled=True)


def spread_out(block, axes, count):
    return exchange(jnp.broadcast_to(block[None], (count,) + block.shape), axes)


def both_ways(value, axes, count):
    pairs = [(2 * i, 2 * ((i + 1) % count)) for i in range(count)]
    pairs += [(2 * i + 1, 2 * ((i - 1) % count) + 1) for i in range(count)]
    return lax.ppermute(value, axes + ("core",), pairs)


def add_products(near_ref, far_ref, weight_refs, acc_ref, first_column=0):
    for block, weight in enumerate(weight_refs):
        columns = pl.ds(first_column + 256 * block, 256)
        for start, rows in ((0, near_ref), (ROWS, far_ref)):
            acc_ref[pl.ds(start, ROWS), columns] += jnp.dot(
                rows[...], weight[...], preferred_element_type=jnp.float32
            )


def times_block(values, block_ref):
    parts = block_ref[...].astype(jnp.float32)
    table = parts[0:64] + parts[64:128] + parts[128:192]
    return lax.dot_general(
        values, table, (((1,), (1,)), ((), ())), precision=PRECISE, preferred_element_type=jnp.float32
    )


def label_rows_of(near_digits, far_digits, starts, tables):
    digits = jnp.concatenate([near_digits[...], far_digits[...]], axis=0).astype(jnp.float32)
    labels = digits[:, 0:1] * 65536.0 + digits[:, 1:2] * 256.0 + digits[:, 2:3]
    ids = lax.broadcasted_iota(jnp.int32, (2 * ROWS, 256), 1)
    rows = jnp.zeros((2 * ROWS, 64), jnp.float32)
    for start, table in zip(starts, tables):
        columns = (ids + start).astype(jnp.float32)
        rows += times_block(jnp.where(labels == columns, 1.0, 0.0), table)
    return rows


def first_kernel(where_ref, near_ref, far_ref, w0, w1, w2, near_digits, far_digits, t0, t1, t2, acc_ref, label_ref):
    @pl.when(pl.program_id(0) == 0)
    def _():
        acc_ref[...] = jnp.zeros_like(acc_ref)
        label_ref[...] = label_rows_of(near_digits, far_digits, [where_ref[3 + i] for i in range(3)], (t0, t1, t2))

    add_products(near_ref, far_ref, (w0, w1, w2), acc_ref)


def last_kernel(
    where_ref, near_ref, far_ref, w0, w1, w2, w3, near3_ref, far3_ref, own3_ref, near_digits, far_digits, t0, t1, t2, t3, begun_ref, label_ref, out_ref, acc_ref
):
    step = pl.program_id(0)

    @pl.when(step == 0)
    def _():
        acc_ref[:, 0:768] = begun_ref[...]
        acc_ref[:, 768:1024] = jnp.zeros((2 * ROWS, 256), jnp.float32)

    add_products(near_ref, far_ref, (w0, w1, w2, w3), acc_ref)
    add_products(near3_ref, far3_ref, (own3_ref,), acc_ref, 768)

    @pl.when(step == STEPS - 1)
    def _():
        logits = acc_ref[...]
        largest = jnp.max(logits, axis=1, keepdims=True)
        exponent = jnp.exp(logits - largest)
        totals = jnp.sum(exponent, axis=1, keepdims=True)
        sums = jnp.zeros((2 * ROWS, 64), jnp.float32)
        for block, table in enumerate((t0, t1, t2, t3)):
            sums += times_block(exponent[:, 256 * block : 256 * block + 256], table)
        label_rows = label_ref[...] + label_rows_of(near_digits, far_digits, [where_ref[6]], [t3])
        left = jnp.concatenate([sums, label_rows], axis=1)
        lane = lax.broadcasted_iota(jnp.int32, (2 * ROWS, 128), 1)
        right = jnp.where(lane == 0, largest, jnp.where(lane == 1, totals, 0.0))
        parity = where_ref[1]
        for start, place in ((0, parity), (ROWS, 1 - parity)):
            out_ref[:, pl.ds(place, 1), :, 0:128] = left[start : start + ROWS].reshape(4, 1, 32, 128)
            out_ref[:, pl.ds(place, 1), :, 128:256] = right[start : start + ROWS].reshape(4, 1, 32, 128)


def merge_kernel(parts_ref, out_ref):
    left, right = parts_ref[:, :, 0:128], parts_ref[:, :, 128:256]
    largest = right[:, :, 0:1]
    top = jnp.max(largest, axis=0, keepdims=True)
    scaled = jnp.exp(largest - top)
    lane = lax.broadcasted_iota(jnp.int32, (1, 8, 128), 2)
    sums = jnp.sum(left * scaled, axis=0, keepdims=True)
    label_rows = jnp.sum(left, axis=0, keepdims=True)
    totals = jnp.sum(right[:, :, 1:2] * scaled, axis=0, keepdims=True)
    left = jnp.where(lane < 64, sums, label_rows)
    right = jnp.where(lane == 0, top, jnp.where(lane == 1, totals, 0.0))
    out_ref[:, :, 0:128] = jnp.broadcast_to(left, (32, 8, 128))
    out_ref[:, :, 128:256] = jnp.broadcast_to(right, (32, 8, 128))


def end_kernel(parts_ref, mapped_ref, even_ref, odd_ref, right_ref, queries_ref, out_ref):
    def precise(first, second):
        return jnp.dot(first, second, precision=PRECISE, preferred_element_type=jnp.float32)

    parts = [parts_ref[:, part].reshape(64, 256) for part in range(4)]
    largest = [part[:, 128:129] for part in parts]
    top = functools.reduce(jnp.maximum, largest)
    scaled = [jnp.exp(value - top) for value in largest]
    totals = sum(part[:, 129:130] * scale for part, scale in zip(parts, scaled))
    sums = sum(part[:, 0:64] * scale for part, scale in zip(parts, scaled))
    projected = sums / totals - sum(part[:, 64:128] for part in parts)
    feature = precise(mapped_ref[...], projected)
    even = precise(precise(even_ref[...], feature), right_ref[...])
    odd = precise(precise(odd_ref[...], feature), right_ref[...])
    flat = jnp.concatenate([even, odd], axis=1)
    products = jnp.zeros((128, 128), jnp.float32)
    for pair in range(32):
        products += queries_ref[:, 128 * pair : 128 * pair + 128] * flat[pair : pair + 1, :]
    lane = lax.broadcasted_iota(jnp.int32, (8, 16), 1)
    scores = jnp.zeros((8, 16), jnp.float32)
    for block in range(16):
        column = jnp.sum(products[8 * block : 8 * block + 8], axis=1, keepdims=True)
        scores = jnp.where(lane == block, column, scores)
    out_ref[...] = scores


def product_specs(blocks, half=0):
    rows = pl.BlockSpec((ROWS, DEPTH), lambda step, where: (0, step))
    weight = pl.BlockSpec((DEPTH, 256), lambda step, where: (where[half] * STEPS + step, 0))
    return [rows, rows] + [weight] * blocks


def side_specs(blocks):
    digits = pl.BlockSpec((ROWS, 128), lambda step, where: (0, 18))
    table = pl.BlockSpec((192, 256), lambda step, where: (24, 0))
    return [digits, digits] + [table] * blocks


def whole(shape):
    return pl.BlockSpec(shape, lambda step, where: (0,) * len(shape))


COST = dict(flops=2 * 256 * 2304 * 1024, bytes_accessed=7_000_000)


def first_products(where, near, far, weights):
    return pl.pallas_call(
        first_kernel,
        out_shape=(jax.ShapeDtypeStruct((256, 768), jnp.float32), jax.ShapeDtypeStruct((256, 64), jnp.float32)),
        grid_spec=pltpu.PrefetchScalarGridSpec(
            num_scalar_prefetch=1,
            grid=(STEPS,),
            in_specs=product_specs(3, 2) + side_specs(3),
            out_specs=(whole((256, 768)), whole((256, 64))),
        ),
        compiler_params=pltpu.CompilerParams(vmem_limit_bytes=24 << 20),
        cost_estimate=pl.CostEstimate(transcendentals=0, **COST),
    )(where, near, far, *weights, near, far, *weights)


def last_products(where, near_x, far_x, weights, near, far, begun, label_rows):
    return pl.pallas_call(
        last_kernel,
        out_shape=jax.ShapeDtypeStruct((4, 2, 32, 256), jnp.float32),
        grid_spec=pltpu.PrefetchScalarGridSpec(
            num_scalar_prefetch=1,
            grid=(STEPS,),
            in_specs=product_specs(4)
            + product_specs(1, 2)
            + side_specs(4)
            + [whole((256, 768)), whole((256, 64))],
            out_specs=whole((4, 2, 32, 256)),
            scratch_shapes=[pltpu.VMEM((256, 1024), jnp.float32)],
        ),
        compiler_params=pltpu.CompilerParams(vmem_limit_bytes=24 << 20),
        cost_estimate=pl.CostEstimate(transcendentals=256 * 1024, **COST),
    )(where, near_x, far_x, *weights, near, far, weights[3], near, far, *weights, begun, label_rows)


def local(hidden, labels, unembed, in_proj, out_proj, left_inv, right_inv, queries):
    core, xl, xh, zl = [lax.axis_index(name) for name in ("core", "xl", "xh", "zl")]
    y = lax.axis_index("yh") * 2 + lax.axis_index("yl")
    rows = 16 * (2 * lax.axis_index("yl") + core)
    z = lax.axis_index("zh") * 2 + zl

    chosen = lax.dynamic_slice(hidden, (rows, 2304 * xl), (16, 2304))
    picked = lax.dynamic_slice(labels, (rows,), (16,))
    digits = jnp.stack([picked // 65536, (picked // 256) % 256, picked % 256], axis=1)
    digits = jnp.pad(digits, ((0, 0), (0, 125))).astype(jnp.bfloat16)
    chosen = jnp.concatenate([chosen, digits], axis=1)
    near = spread_out(chosen, ("zh", "xh"), 8).reshape(ROWS, 2432)

    table = out_proj.T
    high = lax.reduce_precision(table, 8, 7)
    middle = lax.reduce_precision(table - high, 8, 7)
    parts = [part.astype(jnp.bfloat16) for part in (high, middle, table - high - middle)]
    block = jnp.concatenate([unembed] + parts, axis=0)

    query_pair = lax.all_gather(queries[0], "xh", axis=0)
    near, query_pair = lax.optimization_barrier((near, query_pair))
    far = both_ways(near, ("zh", "zl"), 8)
    near_x = both_ways(near, ("xh", "xl"), 4)
    far_x = both_ways(far, ("xh", "xl"), 4)
    moved = both_ways(block, ("yh", "yl"), 8)
    every_query = lax.all_gather(query_pair, ("zh", "zl"), axis=0)
    swapped = lax.ppermute(block, "core", SWAP)
    late, _ = lax.optimization_barrier((moved, far))
    weights = [block, moved, swapped, lax.ppermute(late, "core", SWAP)]

    below, above = ((y + 7) % 8) * 2, ((y + 1) % 8) * 2 + 1
    places = [
        2 * y + core,
        jnp.where(core == 0, below, above),
        2 * y + 1 - core,
        jnp.where(core == 0, above, below),
    ]
    starts = [(((z * 2 + xh) * 2 + xl) * 16 + place) * 256 for place in places]
    where = jnp.stack([1 - xl, zl, xl] + starts)
    mapped = jnp.dot(hidden, in_proj, preferred_element_type=jnp.float32)

    near, near_x = lax.optimization_barrier((near, near_x))
    begun, label_rows = first_products(where, near, far, weights[:3])
    packed = last_products(where, near_x, far_x, weights, near, far, begun, label_rows)
    parts = exchange(packed.reshape(32, 8, 256), ("zh", "zl", "xh", "xl"))
    parts, every_query = lax.optimization_barrier((parts, every_query))
    merged = pl.pallas_call(
        merge_kernel,
        out_shape=jax.ShapeDtypeStruct((32, 8, 256), jnp.float32),
        cost_estimate=pl.CostEstimate(flops=300_000, bytes_accessed=600_000, transcendentals=256),
    )(parts)
    parts = exchange(merged, VOC).reshape(2, 4, 4, 8, 256)
    mapped = jnp.transpose(mapped.reshape(4, 2, 8, 64), (3, 1, 0, 2)).reshape(64, 64)
    scores = pl.pallas_call(
        end_kernel,
        out_shape=jax.ShapeDtypeStruct((8, 16), jnp.float32),
        in_specs=[pl.BlockSpec(memory_space=pltpu.VMEM)] * 6,
        cost_estimate=pl.CostEstimate(flops=2_000_000, bytes_accessed=2_500_000, transcendentals=256),
        compiler_params=pltpu.CompilerParams(vmem_limit_bytes=24 << 20),
    )(parts, mapped, left_inv[0::2], left_inv[1::2], right_inv, every_query.reshape(128, 4096))
    return scores.T[None]


def solution(mesh):
    fine = Mesh(mesh.devices.reshape(4, 2, 2, 2, 4, 2, 2), EVERY)
    in_specs = (
        P(DP, None),
        P(DP),
        P(None, EVERY),
        P(),
        P(EVERY, None),
        P(),
        P(),
        P(DP, VOC, None),
    )
    out_specs = P(DP, None, VOC)
    return jax.shard_map(local, mesh=fine, in_specs=in_specs, out_specs=out_specs, check_vma=False)
```

```python
import functools
import jax
import jax.numpy as jnp
from jax import lax
from jax.experimental import pallas as pl
from jax.experimental.pallas import tpu as pltpu
from jax.sharding import Mesh, PartitionSpec as P

PRECISE = lax.Precision.HIGHEST
EVERY = ("zh", "zl", "xh", "xl", "yh", "yl", "core")
DP = ("zh", "zl", "xh")
VOC = ("xl", "yh", "yl", "core")
SWAP = [(0, 1), (1, 0)]
STEPS = 3
DEPTH = 2304 // STEPS
ROWS = 128


def exchange(blocks, axes):
    return lax.all_to_all(blocks, axes, split_axis=0, concat_axis=0, tiled=True)


def spread_out(block, axes, count):
    return exchange(jnp.broadcast_to(block[None], (count,) + block.shape), axes)


def both_ways(value, axes, count):
    pairs = [(2 * i, 2 * ((i + 1) % count)) for i in range(count)]
    pairs += [(2 * i + 1, 2 * ((i - 1) % count) + 1) for i in range(count)]
    return lax.ppermute(value, axes + ("core",), pairs)


def add_products(near_ref, far_ref, weight_refs, acc_ref, first_column=0):
    for block, weight in enumerate(weight_refs):
        columns = pl.ds(first_column + 256 * block, 256)
        for start, rows in ((0, near_ref), (ROWS, far_ref)):
            acc_ref[pl.ds(start, ROWS), columns] += jnp.dot(
                rows[...], weight[...], preferred_element_type=jnp.float32
            )


def times_block(values, block_ref):
    parts = block_ref[...].astype(jnp.float32)
    table = parts[0:64] + parts[64:128] + parts[128:192]
    return lax.dot_general(
        values, table, (((1,), (1,)), ((), ())), precision=PRECISE, preferred_element_type=jnp.float32
    )


def label_rows_of(near_digits, far_digits, starts, tables):
    digits = jnp.concatenate([near_digits[...], far_digits[...]], axis=0).astype(jnp.float32)
    labels = digits[:, 0:1] * 65536.0 + digits[:, 1:2] * 256.0 + digits[:, 2:3]
    ids = lax.broadcasted_iota(jnp.int32, (2 * ROWS, 256), 1)
    rows = jnp.zeros((2 * ROWS, 64), jnp.float32)
    for start, table in zip(starts, tables):
        columns = (ids + start).astype(jnp.float32)
        rows += times_block(jnp.where(labels == columns, 1.0, 0.0), table)
    return rows


def first_kernel(where_ref, near_ref, far_ref, w0, w1, w2, near_digits, far_digits, t0, t1, t2, acc_ref, label_ref):
    @pl.when(pl.program_id(0) == 0)
    def _():
        acc_ref[...] = jnp.zeros_like(acc_ref)
        label_ref[...] = label_rows_of(near_digits, far_digits, [where_ref[3 + i] for i in range(3)], (t0, t1, t2))

    add_products(near_ref, far_ref, (w0, w1, w2), acc_ref)


def last_kernel(
    where_ref, near_ref, far_ref, w0, w1, w2, w3, near3_ref, far3_ref, own3_ref, near_digits, far_digits, t0, t1, t2, t3, begun_ref, label_ref, out_ref, acc_ref
):
    step = pl.program_id(0)

    @pl.when(step == 0)
    def _():
        acc_ref[:, 0:768] = begun_ref[...]
        acc_ref[:, 768:1024] = jnp.zeros((2 * ROWS, 256), jnp.float32)

    add_products(near_ref, far_ref, (w0, w1, w2, w3), acc_ref)
    add_products(near3_ref, far3_ref, (own3_ref,), acc_ref, 768)

    @pl.when(step == STEPS - 1)
    def _():
        logits = acc_ref[...]
        largest = jnp.max(logits, axis=1, keepdims=True)
        exponent = jnp.exp(logits - largest)
        totals = jnp.sum(exponent, axis=1, keepdims=True)
        sums = jnp.zeros((2 * ROWS, 64), jnp.float32)
        for block, table in enumerate((t0, t1, t2, t3)):
            sums += times_block(exponent[:, 256 * block : 256 * block + 256], table)
        label_rows = label_ref[...] + label_rows_of(near_digits, far_digits, [where_ref[6]], [t3])
        left = jnp.concatenate([sums, label_rows], axis=1)
        lane = lax.broadcasted_iota(jnp.int32, (2 * ROWS, 128), 1)
        right = jnp.where(lane == 0, largest, jnp.where(lane == 1, totals, 0.0))
        parity = where_ref[1]
        for start, place in ((0, parity), (ROWS, 1 - parity)):
            out_ref[:, pl.ds(place, 1), :, 0:128] = left[start : start + ROWS].reshape(4, 1, 32, 128)
            out_ref[:, pl.ds(place, 1), :, 128:256] = right[start : start + ROWS].reshape(4, 1, 32, 128)


def merge_kernel(parts_ref, out_ref):
    left, right = parts_ref[:, :, 0:128], parts_ref[:, :, 128:256]
    largest = right[:, :, 0:1]
    top = jnp.max(largest, axis=0, keepdims=True)
    scaled = jnp.exp(largest - top)
    lane = lax.broadcasted_iota(jnp.int32, (1, 8, 128), 2)
    sums = jnp.sum(left * scaled, axis=0, keepdims=True)
    label_rows = jnp.sum(left, axis=0, keepdims=True)
    totals = jnp.sum(right[:, :, 1:2] * scaled, axis=0, keepdims=True)
    left = jnp.where(lane < 64, sums, label_rows)
    right = jnp.where(lane == 0, top, jnp.where(lane == 1, totals, 0.0))
    out_ref[:, :, 0:128] = jnp.broadcast_to(left, (32, 8, 128))
    out_ref[:, :, 128:256] = jnp.broadcast_to(right, (32, 8, 128))


def end_kernel(parts_ref, mapped_ref, even_ref, odd_ref, right_ref, queries_ref, out_ref):
    def precise(first, second):
        return jnp.dot(first, second, precision=PRECISE, preferred_element_type=jnp.float32)

    parts = [parts_ref[:, part].reshape(64, 256) for part in range(4)]
    largest = [part[:, 128:129] for part in parts]
    top = functools.reduce(jnp.maximum, largest)
    scaled = [jnp.exp(value - top) for value in largest]
    totals = sum(part[:, 129:130] * scale for part, scale in zip(parts, scaled))
    sums = sum(part[:, 0:64] * scale for part, scale in zip(parts, scaled))
    projected = sums / totals - sum(part[:, 64:128] for part in parts)
    feature = precise(mapped_ref[...], projected)
    even = precise(precise(even_ref[...], feature), right_ref[...])
    odd = precise(precise(odd_ref[...], feature), right_ref[...])
    flat = jnp.concatenate([even, odd], axis=1)
    products = jnp.zeros((128, 128), jnp.float32)
    for pair in range(32):
        products += queries_ref[:, 128 * pair : 128 * pair + 128] * flat[pair : pair + 1, :]
    lane = lax.broadcasted_iota(jnp.int32, (8, 16), 1)
    scores = jnp.zeros((8, 16), jnp.float32)
    for block in range(16):
        column = jnp.sum(products[8 * block : 8 * block + 8], axis=1, keepdims=True)
        scores = jnp.where(lane == block, column, scores)
    out_ref[...] = scores


def product_specs(blocks, half=0):
    rows = pl.BlockSpec((ROWS, DEPTH), lambda step, where: (0, step))
    weight = pl.BlockSpec((DEPTH, 256), lambda step, where: (where[half] * STEPS + step, 0))
    return [rows, rows] + [weight] * blocks


def side_specs(blocks):
    digits = pl.BlockSpec((ROWS, 128), lambda step, where: (0, 18))
    table = pl.BlockSpec((192, 256), lambda step, where: (24, 0))
    return [digits, digits] + [table] * blocks


def whole(shape):
    return pl.BlockSpec(shape, lambda step, where: (0,) * len(shape))


COST = dict(flops=2 * 256 * 2304 * 1024, bytes_accessed=7_000_000)


def first_products(where, near, far, weights):
    return pl.pallas_call(
        first_kernel,
        out_shape=(jax.ShapeDtypeStruct((256, 768), jnp.float32), jax.ShapeDtypeStruct((256, 64), jnp.float32)),
        grid_spec=pltpu.PrefetchScalarGridSpec(
            num_scalar_prefetch=1,
            grid=(STEPS,),
            in_specs=product_specs(3, 2) + side_specs(3),
            out_specs=(whole((256, 768)), whole((256, 64))),
        ),
        compiler_params=pltpu.CompilerParams(vmem_limit_bytes=24 << 20),
        cost_estimate=pl.CostEstimate(transcendentals=0, **COST),
    )(where, near, far, *weights, near, far, *weights)


def last_products(where, near_x, far_x, weights, near, far, begun, label_rows):
    return pl.pallas_call(
        last_kernel,
        out_shape=jax.ShapeDtypeStruct((4, 2, 32, 256), jnp.float32),
        grid_spec=pltpu.PrefetchScalarGridSpec(
            num_scalar_prefetch=1,
            grid=(STEPS,),
            in_specs=product_specs(4)
            + product_specs(1, 2)
            + side_specs(4)
            + [whole((256, 768)), whole((256, 64))],
            out_specs=whole((4, 2, 32, 256)),
            scratch_shapes=[pltpu.VMEM((256, 1024), jnp.float32)],
        ),
        compiler_params=pltpu.CompilerParams(vmem_limit_bytes=24 << 20),
        cost_estimate=pl.CostEstimate(transcendentals=256 * 1024, **COST),
    )(where, near_x, far_x, *weights, near, far, weights[3], near, far, *weights, begun, label_rows)


def local(hidden, labels, unembed, in_proj, out_proj, left_inv, right_inv, queries):
    core, xl, xh, zl = [lax.axis_index(name) for name in ("core", "xl", "xh", "zl")]
    y = lax.axis_index("yh") * 2 + lax.axis_index("yl")
    rows = 16 * (2 * lax.axis_index("yl") + core)
    z = lax.axis_index("zh") * 2 + zl

    chosen = lax.dynamic_slice(hidden, (rows, 2304 * xl), (16, 2304))
    picked = lax.dynamic_slice(labels, (rows,), (16,))
    digits = jnp.stack([picked // 65536, (picked // 256) % 256, picked % 256], axis=1)
    digits = jnp.pad(digits, ((0, 0), (0, 125))).astype(jnp.bfloat16)
    chosen = jnp.concatenate([chosen, digits], axis=1)
    near = spread_out(chosen, ("zh", "xh"), 8).reshape(ROWS, 2432)

    table = out_proj.T
    high = lax.reduce_precision(table, 8, 7)
    middle = lax.reduce_precision(table - high, 8, 7)
    parts = [part.astype(jnp.bfloat16) for part in (high, middle, table - high - middle)]
    block = jnp.concatenate([unembed] + parts, axis=0)

    query_pair = lax.all_gather(queries[0], "xh", axis=0)
    near, query_pair = lax.optimization_barrier((near, query_pair))
    far = both_ways(near, ("zh", "zl"), 8)
    near_x = both_ways(near, ("xh", "xl"), 4)
    late, near_x = lax.optimization_barrier((far, near_x))
    far_x = both_ways(late, ("xh", "xl"), 4)
    moved = both_ways(block, ("yh", "yl"), 8)
    every_query = lax.all_gather(query_pair, ("zh", "zl"), axis=0)
    swapped = lax.ppermute(block, "core", SWAP)
    late, _ = lax.optimization_barrier((moved, far))
    weights = [block, moved, swapped, lax.ppermute(late, "core", SWAP)]

    below, above = ((y + 7) % 8) * 2, ((y + 1) % 8) * 2 + 1
    places = [
        2 * y + core,
        jnp.where(core == 0, below, above),
        2 * y + 1 - core,
        jnp.where(core == 0, above, below),
    ]
    starts = [(((z * 2 + xh) * 2 + xl) * 16 + place) * 256 for place in places]
    where = jnp.stack([1 - xl, zl, xl] + starts)
    mapped = jnp.dot(hidden, in_proj, preferred_element_type=jnp.float32)

    begun, label_rows = first_products(where, near, far, weights[:3])
    packed = last_products(where, near_x, far_x, weights, near, far, begun, label_rows)
    parts = exchange(packed.reshape(32, 8, 256), ("zh", "zl", "xh", "xl"))
    parts, every_query = lax.optimization_barrier((parts, every_query))
    merged = pl.pallas_call(
        merge_kernel,
        out_shape=jax.ShapeDtypeStruct((32, 8, 256), jnp.float32),
        cost_estimate=pl.CostEstimate(flops=300_000, bytes_accessed=600_000, transcendentals=256),
    )(parts)
    parts = exchange(merged, VOC).reshape(2, 4, 4, 8, 256)
    mapped = jnp.transpose(mapped.reshape(4, 2, 8, 64), (3, 1, 0, 2)).reshape(64, 64)
    scores = pl.pallas_call(
        end_kernel,
        out_shape=jax.ShapeDtypeStruct((8, 16), jnp.float32),
        in_specs=[pl.BlockSpec(memory_space=pltpu.VMEM)] * 6,
        cost_estimate=pl.CostEstimate(flops=2_000_000, bytes_accessed=2_500_000, transcendentals=256),
        compiler_params=pltpu.CompilerParams(vmem_limit_bytes=24 << 20),
    )(parts, mapped, left_inv[0::2], left_inv[1::2], right_inv, every_query.reshape(128, 4096))
    return scores.T[None]


def solution(mesh):
    fine = Mesh(mesh.devices.reshape(4, 2, 2, 2, 4, 2, 2), EVERY)
    in_specs = (
        P(DP, None),
        P(DP),
        P(None, EVERY),
        P(),
        P(EVERY, None),
        P(),
        P(),
        P(DP, VOC, None),
    )
    out_specs = P(DP, None, VOC)
    return jax.shard_map(local, mesh=fine, in_specs=in_specs, out_specs=out_specs, check_vma=False)
```

```python
import functools
import jax
import jax.numpy as jnp
from jax import lax
from jax.experimental import pallas as pl
from jax.experimental.pallas import tpu as pltpu
from jax.sharding import Mesh, PartitionSpec as P

PRECISE = lax.Precision.HIGHEST
EVERY = ("zh", "zl", "xh", "xl", "yh", "yl", "core")
DP = ("zh", "zl", "xh")
VOC = ("xl", "yh", "yl", "core")
SWAP = [(0, 1), (1, 0)]
STEPS = 3
DEPTH = 2304 // STEPS
ROWS = 128


def exchange(blocks, axes):
    return lax.all_to_all(blocks, axes, split_axis=0, concat_axis=0, tiled=True)


def spread_out(block, axes, count):
    return exchange(jnp.broadcast_to(block[None], (count,) + block.shape), axes)


def both_ways(value, axes, count):
    pairs = [(2 * i, 2 * ((i + 1) % count)) for i in range(count)]
    pairs += [(2 * i + 1, 2 * ((i - 1) % count) + 1) for i in range(count)]
    return lax.ppermute(value, axes + ("core",), pairs)


def add_products(near_ref, far_ref, weight_refs, acc_ref, first_column=0):
    for block, weight in enumerate(weight_refs):
        columns = pl.ds(first_column + 256 * block, 256)
        for start, rows in ((0, near_ref), (ROWS, far_ref)):
            acc_ref[pl.ds(start, ROWS), columns] += jnp.dot(
                rows[...], weight[...], preferred_element_type=jnp.float32
            )


def times_block(values, block_ref):
    parts = block_ref[...].astype(jnp.float32)
    table = parts[0:64] + parts[64:128] + parts[128:192]
    return lax.dot_general(
        values, table, (((1,), (1,)), ((), ())), precision=PRECISE, preferred_element_type=jnp.float32
    )


def label_rows_of(near_digits, far_digits, starts, tables):
    digits = jnp.concatenate([near_digits[...], far_digits[...]], axis=0).astype(jnp.float32)
    labels = digits[:, 0:1] * 65536.0 + digits[:, 1:2] * 256.0 + digits[:, 2:3]
    ids = lax.broadcasted_iota(jnp.int32, (2 * ROWS, 256), 1)
    rows = jnp.zeros((2 * ROWS, 64), jnp.float32)
    for start, table in zip(starts, tables):
        columns = (ids + start).astype(jnp.float32)
        rows += times_block(jnp.where(labels == columns, 1.0, 0.0), table)
    return rows


def first_kernel(where_ref, near_ref, far_ref, w0, w1, w2, near_digits, far_digits, t0, t1, t2, acc_ref, label_ref):
    @pl.when(pl.program_id(0) == 0)
    def _():
        acc_ref[...] = jnp.zeros_like(acc_ref)
        label_ref[...] = label_rows_of(near_digits, far_digits, [where_ref[3 + i] for i in range(3)], (t0, t1, t2))

    add_products(near_ref, far_ref, (w0, w1, w2), acc_ref)


def last_kernel(
    where_ref, near_ref, far_ref, w0, w1, w2, w3, near3_ref, far3_ref, own3_ref, near_digits, far_digits, t0, t1, t2, t3, begun_ref, label_ref, out_ref, acc_ref
):
    step = pl.program_id(0)

    @pl.when(step == 0)
    def _():
        acc_ref[:, 0:768] = begun_ref[...]
        acc_ref[:, 768:1024] = jnp.zeros((2 * ROWS, 256), jnp.float32)

    add_products(near_ref, far_ref, (w0, w1, w2, w3), acc_ref)
    add_products(near3_ref, far3_ref, (own3_ref,), acc_ref, 768)

    @pl.when(step == STEPS - 1)
    def _():
        logits = acc_ref[...]
        largest = jnp.max(logits, axis=1, keepdims=True)
        exponent = jnp.exp(logits - largest)
        totals = jnp.sum(exponent, axis=1, keepdims=True)
        sums = jnp.zeros((2 * ROWS, 64), jnp.float32)
        for block, table in enumerate((t0, t1, t2, t3)):
            sums += times_block(exponent[:, 256 * block : 256 * block + 256], table)
        label_rows = label_ref[...] + label_rows_of(near_digits, far_digits, [where_ref[6]], [t3])
        left = jnp.concatenate([sums, label_rows], axis=1)
        lane = lax.broadcasted_iota(jnp.int32, (2 * ROWS, 128), 1)
        right = jnp.where(lane == 0, largest, jnp.where(lane == 1, totals, 0.0))
        parity = where_ref[1]
        for start, place in ((0, parity), (ROWS, 1 - parity)):
            out_ref[:, pl.ds(place, 1), :, 0:128] = left[start : start + ROWS].reshape(4, 1, 32, 128)
            out_ref[:, pl.ds(place, 1), :, 128:256] = right[start : start + ROWS].reshape(4, 1, 32, 128)


def merge_kernel(parts_ref, out_ref):
    left, right = parts_ref[:, :, 0:128], parts_ref[:, :, 128:256]
    largest = right[:, :, 0:1]
    top = jnp.max(largest, axis=0, keepdims=True)
    scaled = jnp.exp(largest - top)
    lane = lax.broadcasted_iota(jnp.int32, (1, 8, 128), 2)
    sums = jnp.sum(left * scaled, axis=0, keepdims=True)
    label_rows = jnp.sum(left, axis=0, keepdims=True)
    totals = jnp.sum(right[:, :, 1:2] * scaled, axis=0, keepdims=True)
    left = jnp.where(lane < 64, sums, label_rows)
    right = jnp.where(lane == 0, top, jnp.where(lane == 1, totals, 0.0))
    out_ref[:, :, 0:128] = jnp.broadcast_to(left, (32, 8, 128))
    out_ref[:, :, 128:256] = jnp.broadcast_to(right, (32, 8, 128))


def end_kernel(parts_ref, mapped_ref, even_ref, odd_ref, right_ref, queries_ref, out_ref):
    def precise(first, second):
        return jnp.dot(first, second, precision=PRECISE, preferred_element_type=jnp.float32)

    parts = [parts_ref[:, part].reshape(64, 256) for part in range(4)]
    largest = [part[:, 128:129] for part in parts]
    top = functools.reduce(jnp.maximum, largest)
    scaled = [jnp.exp(value - top) for value in largest]
    totals = sum(part[:, 129:130] * scale for part, scale in zip(parts, scaled))
    sums = sum(part[:, 0:64] * scale for part, scale in zip(parts, scaled))
    projected = sums / totals - sum(part[:, 64:128] for part in parts)
    feature = precise(mapped_ref[...], projected)
    even = precise(precise(even_ref[...], feature), right_ref[...])
    odd = precise(precise(odd_ref[...], feature), right_ref[...])
    flat = jnp.concatenate([even, odd], axis=1)
    products = jnp.zeros((128, 128), jnp.float32)
    for pair in range(32):
        products += queries_ref[:, 128 * pair : 128 * pair + 128] * flat[pair : pair + 1, :]
    lane = lax.broadcasted_iota(jnp.int32, (8, 16), 1)
    scores = jnp.zeros((8, 16), jnp.float32)
    for block in range(16):
        column = jnp.sum(products[8 * block : 8 * block + 8], axis=1, keepdims=True)
        scores = jnp.where(lane == block, column, scores)
    out_ref[...] = scores


def product_specs(blocks, half=0):
    rows = pl.BlockSpec((ROWS, DEPTH), lambda step, where: (0, step))
    weight = pl.BlockSpec((DEPTH, 256), lambda step, where: (where[half] * STEPS + step, 0))
    return [rows, rows] + [weight] * blocks


def side_specs(blocks):
    digits = pl.BlockSpec((ROWS, 128), lambda step, where: (0, 18))
    table = pl.BlockSpec((192, 256), lambda step, where: (24, 0))
    return [digits, digits] + [table] * blocks


def whole(shape):
    return pl.BlockSpec(shape, lambda step, where: (0,) * len(shape))


COST = dict(flops=2 * 256 * 2304 * 1024, bytes_accessed=7_000_000)


def first_products(where, near, far, weights):
    return pl.pallas_call(
        first_kernel,
        out_shape=(jax.ShapeDtypeStruct((256, 768), jnp.float32), jax.ShapeDtypeStruct((256, 64), jnp.float32)),
        grid_spec=pltpu.PrefetchScalarGridSpec(
            num_scalar_prefetch=1,
            grid=(STEPS,),
            in_specs=product_specs(3, 2) + side_specs(3),
            out_specs=(whole((256, 768)), whole((256, 64))),
        ),
        compiler_params=pltpu.CompilerParams(vmem_limit_bytes=24 << 20),
        cost_estimate=pl.CostEstimate(transcendentals=0, **COST),
    )(where, near, far, *weights, near, far, *weights)


def last_products(where, near_x, far_x, weights, near, far, begun, label_rows):
    return pl.pallas_call(
        last_kernel,
        out_shape=jax.ShapeDtypeStruct((4, 2, 32, 256), jnp.float32),
        grid_spec=pltpu.PrefetchScalarGridSpec(
            num_scalar_prefetch=1,
            grid=(STEPS,),
            in_specs=product_specs(4)
            + product_specs(1, 2)
            + side_specs(4)
            + [whole((256, 768)), whole((256, 64))],
            out_specs=whole((4, 2, 32, 256)),
            scratch_shapes=[pltpu.VMEM((256, 1024), jnp.float32)],
        ),
        compiler_params=pltpu.CompilerParams(vmem_limit_bytes=24 << 20),
        cost_estimate=pl.CostEstimate(transcendentals=256 * 1024, **COST),
    )(where, near_x, far_x, *weights, near, far, weights[3], near, far, *weights, begun, label_rows)


def local(hidden, labels, unembed, in_proj, out_proj, left_inv, right_inv, queries):
    core, xl, xh, zl = [lax.axis_index(name) for name in ("core", "xl", "xh", "zl")]
    y = lax.axis_index("yh") * 2 + lax.axis_index("yl")
    rows = 16 * (2 * lax.axis_index("yl") + core)
    z = lax.axis_index("zh") * 2 + zl

    chosen = lax.dynamic_slice(hidden, (rows, 2304 * xl), (16, 2304))
    picked = lax.dynamic_slice(labels, (rows,), (16,))
    digits = jnp.stack([picked // 65536, (picked // 256) % 256, picked % 256], axis=1)
    digits = jnp.pad(digits, ((0, 0), (0, 125))).astype(jnp.bfloat16)
    chosen = jnp.concatenate([chosen, digits], axis=1)
    near = spread_out(chosen, ("zh", "xh"), 8).reshape(ROWS, 2432)

    table = out_proj.T
    high = lax.reduce_precision(table, 8, 7)
    middle = lax.reduce_precision(table - high, 8, 7)
    parts = [part.astype(jnp.bfloat16) for part in (high, middle, table - high - middle)]
    block = jnp.concatenate([unembed] + parts, axis=0)

    query_pair = lax.all_gather(queries[0], "xh", axis=0)
    near, query_pair = lax.optimization_barrier((near, query_pair))
    far = both_ways(near, ("zh", "zl"), 8)
    near_x = both_ways(near, ("xh", "xl"), 4)
    far_x = both_ways(far, ("xh", "xl"), 4)
    moved = both_ways(block, ("yh", "yl"), 8)
    every_query = lax.all_gather(query_pair, ("zh", "zl"), axis=0)
    swapped = lax.ppermute(block, "core", SWAP)
    late, _, _ = lax.optimization_barrier((moved, far, near_x))
    weights = [block, moved, swapped, lax.ppermute(late, "core", SWAP)]

    below, above = ((y + 7) % 8) * 2, ((y + 1) % 8) * 2 + 1
    places = [
        2 * y + core,
        jnp.where(core == 0, below, above),
        2 * y + 1 - core,
        jnp.where(core == 0, above, below),
    ]
    starts = [(((z * 2 + xh) * 2 + xl) * 16 + place) * 256 for place in places]
    where = jnp.stack([1 - xl, zl, xl] + starts)
    mapped = jnp.dot(hidden, in_proj, preferred_element_type=jnp.float32)

    begun, label_rows = first_products(where, near, far, weights[:3])
    packed = last_products(where, near_x, far_x, weights, near, far, begun, label_rows)
    parts = exchange(packed.reshape(32, 8, 256), ("zh", "zl", "xh", "xl"))
    parts, every_query = lax.optimization_barrier((parts, every_query))
    merged = pl.pallas_call(
        merge_kernel,
        out_shape=jax.ShapeDtypeStruct((32, 8, 256), jnp.float32),
        cost_estimate=pl.CostEstimate(flops=300_000, bytes_accessed=600_000, transcendentals=256),
    )(parts)
    parts = exchange(merged, VOC).reshape(2, 4, 4, 8, 256)
    mapped = jnp.transpose(mapped.reshape(4, 2, 8, 64), (3, 1, 0, 2)).reshape(64, 64)
    scores = pl.pallas_call(
        end_kernel,
        out_shape=jax.ShapeDtypeStruct((8, 16), jnp.float32),
        in_specs=[pl.BlockSpec(memory_space=pltpu.VMEM)] * 6,
        cost_estimate=pl.CostEstimate(flops=2_000_000, bytes_accessed=2_500_000, transcendentals=256),
        compiler_params=pltpu.CompilerParams(vmem_limit_bytes=24 << 20),
    )(parts, mapped, left_inv[0::2], left_inv[1::2], right_inv, every_query.reshape(128, 4096))
    return scores.T[None]


def solution(mesh):
    fine = Mesh(mesh.devices.reshape(4, 2, 2, 2, 4, 2, 2), EVERY)
    in_specs = (
        P(DP, None),
        P(DP),
        P(None, EVERY),
        P(),
        P(EVERY, None),
        P(),
        P(),
        P(DP, VOC, None),
    )
    out_specs = P(DP, None, VOC)
    return jax.shard_map(local, mesh=fine, in_specs=in_specs, out_specs=out_specs, check_vma=False)
```

```python
import functools
import jax
import jax.numpy as jnp
from jax import lax
from jax.experimental import pallas as pl
from jax.experimental.pallas import tpu as pltpu
from jax.sharding import Mesh, PartitionSpec as P

PRECISE = lax.Precision.HIGHEST
EVERY = ("zh", "zl", "xh", "xl", "yh", "yl", "core")
DP = ("zh", "zl", "xh")
VOC = ("xl", "yh", "yl", "core")
SWAP = [(0, 1), (1, 0)]
STEPS = 2
DEPTH = 2304 // STEPS
ROWS = 128


def exchange(blocks, axes):
    return lax.all_to_all(blocks, axes, split_axis=0, concat_axis=0, tiled=True)


def spread_out(block, axes, count):
    return exchange(jnp.broadcast_to(block[None], (count,) + block.shape), axes)


def both_ways(value, axes, count):
    pairs = [(2 * i, 2 * ((i + 1) % count)) for i in range(count)]
    pairs += [(2 * i + 1, 2 * ((i - 1) % count) + 1) for i in range(count)]
    return lax.ppermute(value, axes + ("core",), pairs)


def add_products(near_ref, far_ref, weight_refs, acc_ref, first_column=0):
    for block, weight in enumerate(weight_refs):
        columns = pl.ds(first_column + 256 * block, 256)
        for start, rows in ((0, near_ref), (ROWS, far_ref)):
            acc_ref[pl.ds(start, ROWS), columns] += jnp.dot(
                rows[...], weight[...], preferred_element_type=jnp.float32
            )


def times_block(values, block_ref):
    parts = block_ref[...].astype(jnp.float32)
    table = parts[0:64] + parts[64:128] + parts[128:192]
    return lax.dot_general(
        values, table, (((1,), (1,)), ((), ())), precision=PRECISE, preferred_element_type=jnp.float32
    )


def label_rows_of(near_digits, far_digits, starts, tables):
    digits = jnp.concatenate([near_digits[...], far_digits[...]], axis=0).astype(jnp.float32)
    labels = digits[:, 0:1] * 65536.0 + digits[:, 1:2] * 256.0 + digits[:, 2:3]
    ids = lax.broadcasted_iota(jnp.int32, (2 * ROWS, 256), 1)
    rows = jnp.zeros((2 * ROWS, 64), jnp.float32)
    for start, table in zip(starts, tables):
        columns = (ids + start).astype(jnp.float32)
        rows += times_block(jnp.where(labels == columns, 1.0, 0.0), table)
    return rows


def first_kernel(where_ref, near_ref, far_ref, w0, w1, w2, near_digits, far_digits, t0, t1, t2, acc_ref, label_ref):
    @pl.when(pl.program_id(0) == 0)
    def _():
        acc_ref[...] = jnp.zeros_like(acc_ref)
        label_ref[...] = label_rows_of(near_digits, far_digits, [where_ref[3 + i] for i in range(3)], (t0, t1, t2))

    add_products(near_ref, far_ref, (w0, w1, w2), acc_ref)


def last_kernel(
    where_ref, near_ref, far_ref, w0, w1, w2, w3, near3_ref, far3_ref, own3_ref, near_digits, far_digits, t0, t1, t2, t3, begun_ref, label_ref, out_ref, acc_ref
):
    step = pl.program_id(0)

    @pl.when(step == 0)
    def _():
        acc_ref[:, 0:768] = begun_ref[...]
        acc_ref[:, 768:1024] = jnp.zeros((2 * ROWS, 256), jnp.float32)

    add_products(near_ref, far_ref, (w0, w1, w2, w3), acc_ref)
    add_products(near3_ref, far3_ref, (own3_ref,), acc_ref, 768)

    @pl.when(step == STEPS - 1)
    def _():
        logits = acc_ref[...]
        largest = jnp.max(logits, axis=1, keepdims=True)
        exponent = jnp.exp(logits - largest)
        totals = jnp.sum(exponent, axis=1, keepdims=True)
        sums = jnp.zeros((2 * ROWS, 64), jnp.float32)
        for block, table in enumerate((t0, t1, t2, t3)):
            sums += times_block(exponent[:, 256 * block : 256 * block + 256], table)
        label_rows = label_ref[...] + label_rows_of(near_digits, far_digits, [where_ref[6]], [t3])
        left = jnp.concatenate([sums, label_rows], axis=1)
        lane = lax.broadcasted_iota(jnp.int32, (2 * ROWS, 128), 1)
        right = jnp.where(lane == 0, largest, jnp.where(lane == 1, totals, 0.0))
        parity = where_ref[1]
        for start, place in ((0, parity), (ROWS, 1 - parity)):
            out_ref[:, pl.ds(place, 1), :, 0:128] = left[start : start + ROWS].reshape(4, 1, 32, 128)
            out_ref[:, pl.ds(place, 1), :, 128:256] = right[start : start + ROWS].reshape(4, 1, 32, 128)


def merge_kernel(parts_ref, out_ref):
    left, right = parts_ref[:, :, 0:128], parts_ref[:, :, 128:256]
    largest = right[:, :, 0:1]
    top = jnp.max(largest, axis=0, keepdims=True)
    scaled = jnp.exp(largest - top)
    lane = lax.broadcasted_iota(jnp.int32, (1, 8, 128), 2)
    sums = jnp.sum(left * scaled, axis=0, keepdims=True)
    label_rows = jnp.sum(left, axis=0, keepdims=True)
    totals = jnp.sum(right[:, :, 1:2] * scaled, axis=0, keepdims=True)
    left = jnp.where(lane < 64, sums, label_rows)
    right = jnp.where(lane == 0, top, jnp.where(lane == 1, totals, 0.0))
    out_ref[:, :, 0:128] = jnp.broadcast_to(left, (32, 8, 128))
    out_ref[:, :, 128:256] = jnp.broadcast_to(right, (32, 8, 128))


def end_kernel(parts_ref, mapped_ref, even_ref, odd_ref, right_ref, queries_ref, out_ref):
    def precise(first, second):
        return jnp.dot(first, second, precision=PRECISE, preferred_element_type=jnp.float32)

    parts = [parts_ref[:, part].reshape(64, 256) for part in range(4)]
    largest = [part[:, 128:129] for part in parts]
    top = functools.reduce(jnp.maximum, largest)
    scaled = [jnp.exp(value - top) for value in largest]
    totals = sum(part[:, 129:130] * scale for part, scale in zip(parts, scaled))
    sums = sum(part[:, 0:64] * scale for part, scale in zip(parts, scaled))
    projected = sums / totals - sum(part[:, 64:128] for part in parts)
    feature = precise(mapped_ref[...], projected)
    even = precise(precise(even_ref[...], feature), right_ref[...])
    odd = precise(precise(odd_ref[...], feature), right_ref[...])
    flat = jnp.concatenate([even, odd], axis=1)
    products = jnp.zeros((128, 128), jnp.float32)
    for pair in range(32):
        products += queries_ref[:, 128 * pair : 128 * pair + 128] * flat[pair : pair + 1, :]
    lane = lax.broadcasted_iota(jnp.int32, (8, 16), 1)
    scores = jnp.zeros((8, 16), jnp.float32)
    for block in range(16):
        column = jnp.sum(products[8 * block : 8 * block + 8], axis=1, keepdims=True)
        scores = jnp.where(lane == block, column, scores)
    out_ref[...] = scores


def product_specs(blocks, half=0):
    rows = pl.BlockSpec((ROWS, DEPTH), lambda step, where: (0, step))
    weight = pl.BlockSpec((DEPTH, 256), lambda step, where: (where[half] * STEPS + step, 0))
    return [rows, rows] + [weight] * blocks


def side_specs(blocks):
    digits = pl.BlockSpec((ROWS, 128), lambda step, where: (0, 18))
    table = pl.BlockSpec((192, 256), lambda step, where: (24, 0))
    return [digits, digits] + [table] * blocks


def whole(shape):
    return pl.BlockSpec(shape, lambda step, where: (0,) * len(shape))


COST = dict(flops=2 * 256 * 2304 * 1024, bytes_accessed=7_000_000)


def first_products(where, near, far, weights):
    return pl.pallas_call(
        first_kernel,
        out_shape=(jax.ShapeDtypeStruct((256, 768), jnp.float32), jax.ShapeDtypeStruct((256, 64), jnp.float32)),
        grid_spec=pltpu.PrefetchScalarGridSpec(
            num_scalar_prefetch=1,
            grid=(STEPS,),
            in_specs=product_specs(3, 2) + side_specs(3),
            out_specs=(whole((256, 768)), whole((256, 64))),
        ),
        compiler_params=pltpu.CompilerParams(vmem_limit_bytes=24 << 20),
        cost_estimate=pl.CostEstimate(transcendentals=0, **COST),
    )(where, near, far, *weights, near, far, *weights)


def last_products(where, near_x, far_x, weights, near, far, begun, label_rows):
    return pl.pallas_call(
        last_kernel,
        out_shape=jax.ShapeDtypeStruct((4, 2, 32, 256), jnp.float32),
        grid_spec=pltpu.PrefetchScalarGridSpec(
            num_scalar_prefetch=1,
            grid=(STEPS,),
            in_specs=product_specs(4)
            + product_specs(1, 2)
            + side_specs(4)
            + [whole((256, 768)), whole((256, 64))],
            out_specs=whole((4, 2, 32, 256)),
            scratch_shapes=[pltpu.VMEM((256, 1024), jnp.float32)],
        ),
        compiler_params=pltpu.CompilerParams(vmem_limit_bytes=24 << 20),
        cost_estimate=pl.CostEstimate(transcendentals=256 * 1024, **COST),
    )(where, near_x, far_x, *weights, near, far, weights[3], near, far, *weights, begun, label_rows)


def local(hidden, labels, unembed, in_proj, out_proj, left_inv, right_inv, queries):
    core, xl, xh, zl = [lax.axis_index(name) for name in ("core", "xl", "xh", "zl")]
    y = lax.axis_index("yh") * 2 + lax.axis_index("yl")
    rows = 16 * (2 * lax.axis_index("yl") + core)
    z = lax.axis_index("zh") * 2 + zl

    chosen = lax.dynamic_slice(hidden, (rows, 2304 * xl), (16, 2304))
    picked = lax.dynamic_slice(labels, (rows,), (16,))
    digits = jnp.stack([picked // 65536, (picked // 256) % 256, picked % 256], axis=1)
    digits = jnp.pad(digits, ((0, 0), (0, 125))).astype(jnp.bfloat16)
    chosen = jnp.concatenate([chosen, digits], axis=1)
    near = spread_out(chosen, ("zh", "xh"), 8).reshape(ROWS, 2432)

    table = out_proj.T
    high = lax.reduce_precision(table, 8, 7)
    middle = lax.reduce_precision(table - high, 8, 7)
    parts = [part.astype(jnp.bfloat16) for part in (high, middle, table - high - middle)]
    block = jnp.concatenate([unembed] + parts, axis=0)

    query_pair = lax.all_gather(queries[0], "xh", axis=0)
    near, query_pair = lax.optimization_barrier((near, query_pair))
    far = both_ways(near, ("zh", "zl"), 8)
    near_x = both_ways(near, ("xh", "xl"), 4)
    far_x = both_ways(far, ("xh", "xl"), 4)
    moved = both_ways(block, ("yh", "yl"), 8)
    every_query = lax.all_gather(query_pair, ("zh", "zl"), axis=0)
    swapped = lax.ppermute(block, "core", SWAP)
    late, _, _ = lax.optimization_barrier((moved, far, near_x))
    weights = [block, moved, swapped, lax.ppermute(late, "core", SWAP)]

    below, above = ((y + 7) % 8) * 2, ((y + 1) % 8) * 2 + 1
    places = [
        2 * y + core,
        jnp.where(core == 0, below, above),
        2 * y + 1 - core,
        jnp.where(core == 0, above, below),
    ]
    starts = [(((z * 2 + xh) * 2 + xl) * 16 + place) * 256 for place in places]
    where = jnp.stack([1 - xl, zl, xl] + starts)
    mapped = jnp.dot(hidden, in_proj, preferred_element_type=jnp.float32)

    begun, label_rows = first_products(where, near, far, weights[:3])
    packed = last_products(where, near_x, far_x, weights, near, far, begun, label_rows)
    parts = exchange(packed.reshape(32, 8, 256), ("zh", "zl", "xh", "xl"))
    parts, every_query = lax.optimization_barrier((parts, every_query))
    merged = pl.pallas_call(
        merge_kernel,
        out_shape=jax.ShapeDtypeStruct((32, 8, 256), jnp.float32),
        cost_estimate=pl.CostEstimate(flops=300_000, bytes_accessed=600_000, transcendentals=256),
    )(parts)
    parts = exchange(merged, VOC).reshape(2, 4, 4, 8, 256)
    mapped = jnp.transpose(mapped.reshape(4, 2, 8, 64), (3, 1, 0, 2)).reshape(64, 64)
    scores = pl.pallas_call(
        end_kernel,
        out_shape=jax.ShapeDtypeStruct((8, 16), jnp.float32),
        in_specs=[pl.BlockSpec(memory_space=pltpu.VMEM)] * 6,
        cost_estimate=pl.CostEstimate(flops=2_000_000, bytes_accessed=2_500_000, transcendentals=256),
        compiler_params=pltpu.CompilerParams(vmem_limit_bytes=24 << 20),
    )(parts, mapped, left_inv[0::2], left_inv[1::2], right_inv, every_query.reshape(128, 4096))
    return scores.T[None]


def solution(mesh):
    fine = Mesh(mesh.devices.reshape(4, 2, 2, 2, 4, 2, 2), EVERY)
    in_specs = (
        P(DP, None),
        P(DP),
        P(None, EVERY),
        P(),
        P(EVERY, None),
        P(),
        P(),
        P(DP, VOC, None),
    )
    out_specs = P(DP, None, VOC)
    return jax.shard_map(local, mesh=fine, in_specs=in_specs, out_specs=out_specs, check_vma=False)
```
